256 devices in a mesh: gx: 4 (over y_hi, core), yz: 64 (over y_lo, z, x).
Axes of the slice: x: 4, y: 4 (y_hi: 2, y_lo: 2; y = y_hi * 2 + y_lo), z: 8, core: 2. Of those that a mesh axis runs over, the one named last changes fastest.
Arguments:
- terminal_adjoint: float32 [4, 32, 64, 64, 128], P(None, 'gx', None, 'yz'), may hold values from -6 to 6
- diffusivity: float32 [4, 32, 64, 64, 128], P(None, 'gx', None, 'yz'), may hold values from 0.02 to 0.08
- velocity: float32 [3, 32, 64, 64, 128], P(None, 'gx', None, 'yz'), may hold values from -1 to 1
- charge_modes: float32 [32, 64, 16, 512], P('gx', 'yz'), may hold values from -0.6 to 0.6
Outputs:
- adjoint: float32 [4, 32, 64, 64, 128], P(None, 'gx', None, 'yz')
The draws below stay inside these ranges and needn't reach their ends.
All inputs are finite; a program needn't handle non-finite values.
Results may differ from the reference program's by a relative error of at most 0.00005.
Values sent between devices are 32-bit elements; how exact they have to be, the bound alone decides.
A program may use at most 64 MiB of HBM per device.

```python
import math
import jax
import jax.numpy as jnp
from jax import lax

SPECIES = 4
PZ = 4
BZ = 128
STEPS = 3
PY = 16
BY = 64
NBLK = 64
NX = 32
NY = 1024
NZ = 512


def block_levels(rng, extent, split, low, largest):
    factor_of = 1.0
    for position, shards_of in split:
        draws = jax.random.uniform(jax.random.fold_in(jax.random.fold_in(rng, 6), position), (shards_of,), jnp.float32, low / len(split), largest / len(split))
        factor_of = factor_of * jnp.repeat(jnp.exp(draws), extent[position] // shards_of).reshape((-1,) + (1,) * (len(extent) - 1 - position))
    return factor_of


def centred(rng, extent, scale, most, cuts=(), held_as=jnp.bfloat16):
    result = jax.random.normal(rng, extent, jnp.float32) * scale
    if len(cuts) > 0:
        result = block_levels(rng, extent, cuts, -0.22, 0.18) * result
    return jnp.clip(result, min=-most, max=most).astype(held_as)


def setup_inputs(seed: int = 0) -> dict:
    streams_of = jax.random.split(jax.random.key(seed), 5)
    return {
        "terminal_adjoint": centred(streams_of[0], (SPECIES, NX, BY, NBLK, BZ), 1.0, 6.0, ((1, 4), (3, 64)), jnp.float32),
        "diffusivity": jnp.clip(jnp.exp(math.log(0.08) - 1.3862944 * jax.random.uniform(streams_of[1], (SPECIES, NX, BY, NBLK, BZ), jnp.float32) ** block_levels(streams_of[1], (SPECIES, NX, BY, NBLK, BZ), ((1, 4), (3, 64)), -0.2, 0.2)), 0.02, 0.08),
        "velocity": centred(streams_of[2], (3, NX, BY, NBLK, BZ), 0.2, 1.0, ((1, 4), (3, 64)), jnp.float32),
        "charge_modes": centred(streams_of[3], (NX, BY, PY, NZ), 0.1, 0.6, ((0, 4), (1, 64)), jnp.float32),
    }


VALENCE = (1.0, -1.0, 2.0, -1.0)
SCREEN = 1.0


def column_table(length):
    half = length // 2
    modes = lax.iota(jnp.int32, half)[:, None]
    cells = lax.iota(jnp.int32, length)[None, :]
    phase = ((modes * cells) % length).astype(jnp.float32)
    angle = phase * (2.0 * math.pi / length)
    theta = modes.astype(jnp.float32) * (2.0 * math.pi / length)
    green = 1.0 / (1.0 + SCREEN * theta * theta)
    return jnp.concatenate([jnp.cos(angle) * green, jnp.sin(angle) * green], 0)


def to_grid(array):
    count = array.shape[0]
    shaped = array.reshape(count, NX, BY, PZ, PY, BZ)
    return jnp.transpose(shaped, (0, 1, 4, 2, 3, 5)).reshape(count, NX, NY, NZ)


def from_grid(array):
    count = array.shape[0]
    shaped = array.reshape(count, NX, PY, BY, PZ, BZ)
    return jnp.transpose(shaped, (0, 1, 3, 4, 2, 5)).reshape(count, NX, BY, NBLK, BZ)


def neighbours(grid):
    padded = jnp.pad(grid, 1)
    return (padded[2:, 1:-1, 1:-1], padded[:-2, 1:-1, 1:-1],
            padded[1:-1, 2:, 1:-1], padded[1:-1, :-2, 1:-1],
            padded[1:-1, 1:-1, 2:], padded[1:-1, 1:-1, :-2])


def advance(adjoint, diffusion, velocity, slopes, valence):
    x_plus, x_minus, y_plus, y_minus, z_plus, z_minus = neighbours(adjoint)
    spread = ((x_plus + x_minus) + (y_plus + y_minus)) + (z_plus + z_minus) - 6.0 * adjoint
    drift = 0.25 * valence * diffusion
    change = diffusion * spread
    change = change + (0.5 * velocity[0] - drift * slopes[0]) * (x_plus - x_minus)
    change = change + (0.5 * velocity[1] - drift * slopes[1]) * (y_plus - y_minus)
    change = change + (0.5 * velocity[2] - drift * slopes[2]) * (z_plus - z_minus)
    return adjoint + change


def reference(terminal_adjoint, diffusivity, velocity, charge_modes):
    table = column_table(NZ)
    columns = jnp.transpose(charge_modes, (0, 2, 1, 3)).reshape(NX * NY, NZ)
    potential = jnp.dot(columns, table, preferred_element_type=jnp.float32,
                        precision=lax.Precision.HIGHEST).reshape(NX, NY, NZ)
    near = neighbours(potential)
    slopes = (near[0] - near[1], near[2] - near[3], near[4] - near[5])
    adjoint_grid = to_grid(terminal_adjoint)
    diffusion_grid = to_grid(diffusivity)
    velocity_grid = to_grid(velocity)
    results = []
    for species in range(SPECIES):
        adjoint = adjoint_grid[species]
        for repeat in range(STEPS):
            adjoint = advance(adjoint, diffusion_grid[species], velocity_grid, slopes, VALENCE[species])
        results.append(adjoint)
    return from_grid(jnp.stack(results, 0))
```

```python
import functools
import math

import jax
import jax.numpy as jnp
import ml_dtypes
import numpy as np
from jax import lax
from jax.experimental import pallas as pl
from jax.experimental.pallas import tpu as pltpu
from jax.sharding import PartitionSpec as P

SPECIES = 4
STEPS = 3
SCREEN = 1.0
MESH = pl.DeviceIdType.MESH

PZ, PY = 4, 16
NYZ = PZ * PY
BX, BY, BZ = 8, 64, 128
MODES = 512
TOP, ROWS = 8, 80
OWN = slice(TOP, TOP + BY)
F32, BF16 = jnp.float32, jnp.bfloat16


def base_table():
    half = MODES // 2
    modes = np.arange(half)[:, None]
    cells = np.arange(BZ)[None, :]
    angle = (modes * cells % MODES) * (2.0 * math.pi / MODES)
    theta = modes * (2.0 * math.pi / MODES)
    green = 1.0 / (1.0 + SCREEN * theta * theta)
    table = np.concatenate([np.cos(angle) * green, np.sin(angle) * green], 0)
    high = table.astype(np.float32).astype(ml_dtypes.bfloat16)
    low = (table - high.astype(np.float64)).astype(ml_dtypes.bfloat16)
    return high, low


def quarter_turned(a, b, turns):
    if turns == 0:
        return a, b
    k = lax.broadcasted_iota(jnp.int32, a.shape, 1)
    odd = (k & 1) == 1
    if turns == 2:
        return jnp.where(odd, -a, a), jnp.where(odd, -b, b)
    third = (k & 2) == 2
    if turns == 3:
        third = third != odd
    cos_part = jnp.where(odd, b, a)
    sin_part = jnp.where(odd, a, b)
    cos_part = jnp.where(third, -cos_part, cos_part)
    sin_part = jnp.where(third != odd, -sin_part, sin_part)
    return cos_part, sin_part


def lanes():
    return lax.broadcasted_iota(jnp.int32, (8, BZ), 1)


def pack_plane(plane, x):
    lane = lanes()
    parts = [plane[8 * r : 8 * r + 8] for r in range(8)]
    width = 2
    while len(parts) > 1:
        moved = (lane >= width - 1) & (lane < 2 * width - 1)
        parts = [
            jnp.where(moved, pltpu.roll(right, width, 1), left)
            for left, right in zip(parts[::2], parts[1::2])
        ]
        width *= 2
    whole = parts[0]
    if x > 0:
        whole = pltpu.roll(whole, 16 * x, 1)
    return whole


def merged(packed, whole, x):
    lane = lanes()
    if x == 0:
        return whole
    return jnp.where((lane >= 16 * x - 1) & (lane < 16 * x + 15), whole, packed)


def unpack_plane(packed, x):
    if x > 0:
        packed = pltpu.roll(packed, BZ - 16 * x, 1)
    return jnp.concatenate(
        [packed] + [pltpu.roll(packed, BZ - 2 * r, 1) for r in range(1, 8)], 0
    )


def slab_kernel(
    lam_hbm, dif_hbm, vel_hbm, cm_hbm, high_hbm, low_hbm, out_hbm,
    l0, l1, l2, l3, dif, vel, drift, slope, pot, cm, high, low,
    product, sendbuf, recv, y_out, y_in, z_out, z_in,
    load_sem, a2a_send, a2a_recv, halo_send, halo_recv,
):
    gx = lax.axis_index("gx")
    me = lax.axis_index("yz")
    ngx = lax.axis_size("gx")
    p = lax.rem(me, PY)
    zb = lax.div(me, PY)
    has = {
        "x+": gx < ngx - 1, "x-": gx > 0,
        "y+": p < PY - 1, "y-": p > 0,
        "z+": zb < PZ - 1, "z-": zb > 0,
    }
    ids = {
        "x+": {"gx": gx + 1}, "x-": {"gx": gx - 1},
        "y+": {"yz": me + 1}, "y-": {"yz": me - 1},
        "z+": {"yz": me + PY}, "z-": {"yz": me - PY},
    }
    ways = ("x+", "x-", "y+", "y-", "z+", "z-")
    back = {"x+": "x-", "x-": "x+", "y+": "y-", "y-": "y+", "z+": "z-", "z-": "z+"}

    own = (slice(None), slice(1, 1 + BX), OWN)
    loads = [
        pltpu.make_async_copy(cm_hbm, cm, load_sem.at[0]),
        pltpu.make_async_copy(high_hbm, high, load_sem.at[1]),
        pltpu.make_async_copy(low_hbm, low, load_sem.at[2]),
        pltpu.make_async_copy(lam_hbm, l0.at[:, pl.ds(1, BX), pl.ds(TOP, BY), :], load_sem.at[3]),
        pltpu.make_async_copy(dif_hbm, dif, load_sem.at[4]),
        pltpu.make_async_copy(vel_hbm, vel, load_sem.at[5]),
    ]
    for load in loads:
        load.start()

    barrier = pltpu.get_barrier_semaphore()

    @pl.loop(1, NYZ)
    def _(k):
        pl.semaphore_signal(
            barrier, inc=1, device_id={"yz": lax.rem(me + k, NYZ)}, device_id_type=MESH
        )

    for way in ("x+", "x-"):
        @pl.when(has[way])
        def _():
            pl.semaphore_signal(barrier, inc=1, device_id=ids[way], device_id_type=MESH)

    zero = jnp.zeros((BY, BZ), F32)

    @pl.when(jnp.logical_not(has["x-"]))
    def _():
        for ref in (l0, l1, l2):
            for s in range(SPECIES):
                ref[s, 0, OWN, :] = zero
        pot[0, 0, OWN, :] = zero

    @pl.when(jnp.logical_not(has["x+"]))
    def _():
        for ref in (l0, l1, l2):
            for s in range(SPECIES):
                ref[s, BX + 1, OWN, :] = zero
        pot[0, BX + 1, OWN, :] = zero

    for load in loads[:3]:
        load.wait()
    charge = cm[...].reshape(BX * PY, MODES)
    a, b = charge[:, : MODES // 2], charge[:, MODES // 2 :]
    dot = functools.partial(jnp.dot, preferred_element_type=F32)
    for turns in range(PZ):
        total = None
        for half, part in enumerate(quarter_turned(a, b, turns)):
            rows = slice(half * MODES // 2, (half + 1) * MODES // 2)
            part_high = part.astype(BF16)
            part_low = (part - part_high.astype(F32)).astype(BF16)
            term = dot(part_high, high[rows, :]) + (
                dot(part_low, high[rows, :]) + dot(part_high, low[rows, :])
            )
            total = term if total is None else total + term
        product[...] = total
        for q in range(PY):
            sendbuf[pl.ds((turns * PY + q) * BX, BX), :] = product[pl.ds(q, BX, stride=PY), :]

    pl.semaphore_wait(
        barrier,
        NYZ - 1 + has["x+"].astype(jnp.int32) + has["x-"].astype(jnp.int32),
    )

    def tile(ref, index):
        return ref.at[pl.ds(pl.multiple_of(index * BX, BX), BX), :]

    @pl.loop(1, NYZ)
    def _(k):
        peer = lax.rem(me + k, NYZ)
        pltpu.make_async_remote_copy(
            src_ref=tile(sendbuf, peer),
            dst_ref=tile(recv, me),
            send_sem=a2a_send,
            recv_sem=a2a_recv,
            device_id={"yz": peer},
            device_id_type=MESH,
        ).start()

    mine = pl.ds(pl.multiple_of(me * BX, BX), BX)
    recv[mine, :] = sendbuf[mine, :]

    def halo_copy(stage, way, fields, y_src=None):
        n = fields.shape[0]
        number = ways.index(way)
        if way == "x+":
            src = fields.at[:, BX, pl.ds(TOP, BY), :]
            dst = fields.at[:, 0, pl.ds(TOP, BY), :]
        elif way == "x-":
            src = fields.at[:, 1, pl.ds(TOP, BY), :]
            dst = fields.at[:, BX + 1, pl.ds(TOP, BY), :]
        elif way[0] == "y":
            src = y_out.at[stage, number - 2, pl.ds(0, n)]
            dst = y_in.at[stage, number - 2, pl.ds(0, n)]
        else:
            src = z_out.at[stage, pl.ds(0, n)]
            dst = z_in.at[stage, number - 4, pl.ds(0, n)]
        return pltpu.make_async_remote_copy(
            src_ref=src, dst_ref=dst,
            send_sem=halo_send.at[stage, number],
            recv_sem=halo_recv.at[stage, number],
            device_id=ids[way], device_id_type=MESH,
        )

    def start(stage, fields, which=ways):
        for way in which:
            @pl.when(has[way])
            def _():
                halo_copy(stage, way, fields).start()

    def receive(stage, fields, which=ways):
        for way in which:
            @pl.when(has[back[way]])
            def _():
                halo_copy(stage, way, fields).wait_recv()

    def finish(stage, fields):
        for way in ways:
            @pl.when(has[way])
            def _():
                halo_copy(stage, way, fields).wait_send()

    def stage_rims(stage, s, planes, fields):
        packed = None
        for x in range(BX):
            plane = planes(x)
            y_out[stage, 0, s, x : x + 1, :] = plane[BY - 1 :]
            y_out[stage, 1, s, x : x + 1, :] = plane[:1]
            packed = merged(packed, pack_plane(plane, x), x)
        z_out[stage, s] = packed

    def place_rims(stage, s, fields):
        low_rows = jnp.where(has["y-"], y_in[stage, 0, s], 0.0)
        high_rows = jnp.where(has["y+"], y_in[stage, 1, s], 0.0)
        for x in range(BX):
            fields[s, x + 1, TOP - 1 : TOP, :] = low_rows[x : x + 1]
            fields[s, x + 1, TOP + BY : TOP + BY + 1, :] = high_rows[x : x + 1]
        below = jnp.where(has["z-"], z_in[stage, 0, s], 0.0)
        above = jnp.where(has["z+"], z_in[stage, 1, s], 0.0)
        even = (lanes() & 1) == 0
        return jnp.where(even, pltpu.roll(below, 1, 1), pltpu.roll(above, BZ - 1, 1))

    lane = lax.broadcasted_iota(jnp.int32, (BY, BZ), 1)

    def near(fields, s, x, packed):
        centre = fields[s, x + 1, OWN, :]
        edge = unpack_plane(packed, x)
        z_plus = jnp.where(lane == BZ - 1, edge, pltpu.roll(centre, BZ - 1, 1))
        z_minus = jnp.where(lane == 0, edge, pltpu.roll(centre, 1, 1))
        return (
            centre,
            fields[s, x + 2, OWN, :], fields[s, x, OWN, :],
            fields[s, x + 1, TOP + 1 : TOP + BY + 1, :], fields[s, x + 1, TOP - 1 : TOP + BY - 1, :],
            z_plus, z_minus,
        )

    for load in loads[3:]:
        load.wait()

    @pl.loop(0, SPECIES)
    def _(s):
        stage_rims(0, s, lambda x: l0[s, x + 1, OWN, :], l0)

    start(0, l0)

    pltpu.make_async_copy(
        recv.at[pl.ds(0, (NYZ - 1) * BX), :], recv.at[pl.ds(0, (NYZ - 1) * BX), :], a2a_recv
    ).wait()
    y_out[1, 0, 0] = recv[pl.ds((BY - 1) * BX, BX), :]
    y_out[1, 1, 0] = recv[pl.ds(0, BX), :]
    start(1, pot, ("y+", "y-"))
    packed = None
    for x in (0, BX - 1):
        pot[0, x + 1, OWN, :] = recv[pl.ds(x, BY, stride=BX), :]
    start(1, pot, ("x+", "x-"))
    for x in range(1, BX - 1):
        pot[0, x + 1, OWN, :] = recv[pl.ds(x, BY, stride=BX), :]
    for x in range(BX):
        packed = merged(packed, pack_plane(pot[0, x + 1, OWN, :], x), x)
    z_out[1, 0] = packed
    start(1, pot, ("z+", "z-"))
    receive(1, pot)
    packed = place_rims(1, 0, pot)
    for x in range(BX):
        _, x_plus, x_minus, y_plus, y_minus, z_plus, z_minus = near(pot, 0, x, packed)
        slope[0, x] = x_plus - x_minus
        slope[1, x] = y_plus - y_minus
        slope[2, x] = z_plus - z_minus

    fields = (l0, l1, l2, l3)
    stages = (0, 2, 3)
    for step in range(STEPS):
        now, later, stage = fields[step], fields[step + 1], stages[step]
        receive(stage, now)

        @pl.loop(0, SPECIES)
        def _(s):
            valence = jnp.where(s == 0, 1.0, jnp.where(s == 2, 2.0, -1.0)).astype(F32)
            packed = place_rims(stage, s, now)
            out = None
            for x in range(BX):
                centre, x_plus, x_minus, y_plus, y_minus, z_plus, z_minus = near(now, s, x, packed)
                diffusion = dif[s, x]
                if step == 0:
                    scaled = (0.25 * valence) * diffusion
                    along = [0.5 * vel[axis, x] - scaled * slope[axis, x] for axis in range(3)]
                    for axis in range(3):
                        drift[axis, s, x] = along[axis]
                else:
                    along = [drift[axis, s, x] for axis in range(3)]
                spread = x_plus + x_minus + (y_plus + y_minus) + (z_plus + z_minus) - 6.0 * centre
                change = diffusion * spread
                change = change + along[0] * (x_plus - x_minus)
                change = change + along[1] * (y_plus - y_minus)
                change = change + along[2] * (z_plus - z_minus)
                new = centre + change
                if step == STEPS - 1:
                    later[s, x] = new
                else:
                    later[s, x + 1, OWN, :] = new
                    y_out[stages[step + 1], 0, s, x : x + 1, :] = new[BY - 1 :]
                    y_out[stages[step + 1], 1, s, x : x + 1, :] = new[:1]
                    out = merged(out, pack_plane(new, x), x)
            if step < STEPS - 1:
                z_out[stages[step + 1], s] = out

        if step < STEPS - 1:
            start(stages[step + 1], later)

    store = pltpu.make_async_copy(l3, out_hbm, load_sem.at[0])
    store.start()

    pltpu.make_async_copy(
        sendbuf.at[pl.ds(0, (NYZ - 1) * BX), :], sendbuf.at[pl.ds(0, (NYZ - 1) * BX), :], a2a_send
    ).wait()
    for stage, ref in ((0, l0), (1, pot), (2, l1), (3, l2)):
        finish(stage, ref)
    store.wait()


def body(terminal_adjoint, diffusivity, velocity, charge_modes):
    high, low = base_table()
    brick = (SPECIES, BX, BY, BZ)
    padded = (SPECIES, BX + 2, ROWS, BZ)
    anywhere = pl.BlockSpec(memory_space=pl.ANY)
    out = pl.pallas_call(
        slab_kernel,
        out_shape=jax.ShapeDtypeStruct(brick, F32),
        in_specs=[anywhere] * 6,
        out_specs=anywhere,
        scratch_shapes=[
            pltpu.VMEM(padded, F32), pltpu.VMEM(padded, F32), pltpu.VMEM(padded, F32),
            pltpu.VMEM(brick, F32),
            pltpu.VMEM(brick, F32),
            pltpu.VMEM((3, BX, BY, BZ), F32),
            pltpu.VMEM((3,) + brick, F32),
            pltpu.VMEM((3, BX, BY, BZ), F32),
            pltpu.VMEM((1, BX + 2, ROWS, BZ), F32),
            pltpu.VMEM((BX, PY, MODES), F32),
            pltpu.VMEM((MODES, BZ), BF16), pltpu.VMEM((MODES, BZ), BF16),
            pltpu.VMEM((BX * PY, BZ), F32),
            pltpu.VMEM((NYZ * BX, BZ), F32),
            pltpu.VMEM((NYZ * BX, BZ), F32),
            pltpu.VMEM((4, 2, SPECIES, BX, BZ), F32),
            pltpu.VMEM((4, 2, SPECIES, BX, BZ), F32),
            pltpu.VMEM((4, SPECIES, 8, BZ), F32),
            pltpu.VMEM((4, 2, SPECIES, 8, BZ), F32),
            pltpu.SemaphoreType.DMA((6,)),
            pltpu.SemaphoreType.DMA,
            pltpu.SemaphoreType.DMA,
            pltpu.SemaphoreType.DMA((4, 6)),
            pltpu.SemaphoreType.DMA((4, 6)),
        ],
        compiler_params=pltpu.CompilerParams(
            collective_id=0, has_side_effects=True, vmem_limit_bytes=60 * 1024 * 1024
        ),
    )(
        terminal_adjoint.reshape(brick),
        diffusivity.reshape(brick),
        velocity.reshape((3,) + brick[1:]),
        charge_modes.reshape(BX, PY, MODES),
        jnp.asarray(high),
        jnp.asarray(low),
    )
    return out.reshape(terminal_adjoint.shape)


def solution(mesh):
    return jax.shard_map(
        body,
        mesh=mesh,
        in_specs=(
            P(None, "gx", None, "yz", None),
            P(None, "gx", None, "yz", None),
            P(None, "gx", None, "yz", None),
            P("gx", "yz", None, None),
        ),
        out_specs=P(None, "gx", None, "yz", None),
        check_vma=False,
    )
```

```python
import functools
import math

import jax
import jax.numpy as jnp
import ml_dtypes
import numpy as np
from jax import lax
from jax.experimental import pallas as pl
from jax.experimental.pallas import tpu as pltpu
from jax.sharding import PartitionSpec as P

SPECIES = 4
STEPS = 3
SCREEN = 1.0
MESH = pl.DeviceIdType.MESH

PZ, PY = 4, 16
NYZ = PZ * PY
BX, BY, BZ = 8, 64, 128
MODES = 512
TOP, ROWS = 8, 80
TILE = BX + 1
ORDER = (0, BX - 1) + tuple(range(1, BX - 1))
PLACE = {x: row for row, x in enumerate(ORDER)}
FACE = 2
LOW, HIGH = NYZ, NYZ + 1
HALF = 32
F32, BF16 = jnp.float32, jnp.bfloat16


def base_table():
    half = MODES // 2
    modes = np.arange(half)[:, None]
    cells = np.arange(BZ)[None, :]
    angle = (modes * cells % MODES) * (2.0 * math.pi / MODES)
    theta = modes * (2.0 * math.pi / MODES)
    green = 1.0 / (1.0 + SCREEN * theta * theta)
    table = np.concatenate([np.cos(angle) * green, np.sin(angle) * green], 0)
    high = table.astype(np.float32).astype(ml_dtypes.bfloat16)
    low = (table - high.astype(np.float64)).astype(ml_dtypes.bfloat16)
    return high, low


def quarter_turned(a, b, turns):
    if turns == 0:
        return a, b
    k = lax.broadcasted_iota(jnp.int32, a.shape, 1)
    odd = (k & 1) == 1
    if turns == 2:
        return jnp.where(odd, -a, a), jnp.where(odd, -b, b)
    third = (k & 2) == 2
    if turns == 3:
        third = third != odd
    cos_part = jnp.where(odd, b, a)
    sin_part = jnp.where(odd, a, b)
    cos_part = jnp.where(third, -cos_part, cos_part)
    sin_part = jnp.where(third != odd, -sin_part, sin_part)
    return cos_part, sin_part


def lanes():
    return lax.broadcasted_iota(jnp.int32, (8, BZ), 1)


def pack_plane(plane, x):
    lane = lanes()
    parts = [plane[8 * r : 8 * r + 8] for r in range(8)]
    width = 2
    while len(parts) > 1:
        moved = (lane >= width - 1) & (lane < 2 * width - 1)
        parts = [
            jnp.where(moved, pltpu.roll(right, width, 1), left)
            for left, right in zip(parts[::2], parts[1::2])
        ]
        width *= 2
    whole = parts[0]
    if x > 0:
        whole = pltpu.roll(whole, 16 * x, 1)
    return whole


def merged(packed, whole, x):
    lane = lanes()
    if x == 0:
        return whole
    return jnp.where((lane >= 16 * x - 1) & (lane < 16 * x + 15), whole, packed)


def unpack_plane(packed, x):
    lane = lanes()
    rim = (lane == 0) | (lane == BZ - 1)
    shifts = [(BZ - 16 * x - 2 * r) % BZ for r in range(8)]
    moved = [pltpu.roll(packed, shift, 1) if shift else packed for shift in shifts]
    return jnp.concatenate([jnp.where(rim, part, 0.0) for part in moved], 0)


def padded_row(x):
    return (x + 1) * ROWS + TOP


def slab_kernel(
    lam_hbm, dif_hbm, vel_hbm, cm_hbm, high_hbm, low_hbm, l3,
    l0, l1, l2, dif, vel, along, base, grad, slope, pot, cm, high, low,
    product, sendbuf, recv, x_in, y_out, y_in, z_out, z_in,
    load_sem, lam_sem, store_sem, a2a_send, a2a_recv, edge_send, edge_recv, halo_send, halo_recv,
):
    gx = lax.axis_index("gx")
    me = lax.axis_index("yz")
    ngx = lax.axis_size("gx")
    p = lax.rem(me, PY)
    zb = lax.div(me, PY)
    mx, mz, my = lax.rem(me, 4), lax.rem(lax.div(me, 4), 8), lax.div(me, 32)
    has = {
        "x+": gx < ngx - 1, "x-": gx > 0,
        "y+": p < PY - 1, "y-": p > 0,
        "z+": zb < PZ - 1, "z-": zb > 0,
    }
    ids = {
        "x+": {"gx": gx + 1}, "x-": {"gx": gx - 1},
        "y+": {"yz": me + 1}, "y-": {"yz": me - 1},
        "z+": {"yz": me + PY}, "z-": {"yz": me - PY},
    }
    ways = ("z+", "z-", "x+", "x-", "y+", "y-")
    back = {"x+": "x-", "x-": "x+", "y+": "y-", "y-": "y+", "z+": "z-", "z-": "z+"}

    def partners(act):
        @pl.loop(0, 8)
        def _(j):
            step = lax.div(j + 1, 2)
            dz = 4 + jnp.where(lax.rem(j, 2) == 0, -step, step)
            z = lax.rem(mz + dz + 8, 8)
            for dx in (2, 1, 3, 0):
                for dy in (1, 0):
                    x = lax.rem(mx + dx, 4) if dx else mx
                    y = 1 - my if dy else my
                    peer = (y * 8 + z) * 4 + x
                    if dx or dy:
                        act(peer)
                    else:
                        pl.when(j < 7)(functools.partial(act, peer))

    barrier = pltpu.get_barrier_semaphore()
    partners(
        lambda peer: pl.semaphore_signal(
            barrier, inc=1, device_id={"yz": peer}, device_id_type=MESH
        )
    )
    for way in ("x+", "x-"):
        @pl.when(has[way])
        def _():
            pl.semaphore_signal(barrier, inc=1, device_id=ids[way], device_id_type=MESH)

    loads = [
        pltpu.make_async_copy(cm_hbm, cm, load_sem.at[0]),
        pltpu.make_async_copy(high_hbm, high, load_sem.at[1]),
        pltpu.make_async_copy(low_hbm, low, load_sem.at[2]),
        pltpu.make_async_copy(dif_hbm, dif, load_sem.at[3]),
        pltpu.make_async_copy(vel_hbm, vel, load_sem.at[4]),
    ]
    lam_loads = [
        pltpu.make_async_copy(lam_hbm.at[:, x], l0.at[:, pl.ds(padded_row(x), BY), :], lam_sem.at[x])
        for x in range(BX)
    ]
    for load in loads[:3] + lam_loads + loads[3:]:
        load.start()

    zero = jnp.zeros((BY, BZ), F32)
    line = jnp.zeros((BX, BZ), F32)
    for ref in (l0, l1, l2):
        @pl.loop(0, SPECIES)
        def _(s):
            ref[s, TOP : TOP + BY, :] = zero
            ref[s, padded_row(BX) : padded_row(BX) + BY, :] = zero
            ref[s, pl.ds(padded_row(0) - 1, BX, stride=ROWS), :] = line
            ref[s, pl.ds(padded_row(0) + BY, BX, stride=ROWS), :] = line

    for side, way in enumerate(("-", "+")):
        @pl.when(jnp.logical_not(has["x" + way]))
        def _():
            for stage in range(STEPS):
                for s in range(SPECIES):
                    x_in[stage, side, s] = zero
            face = TOP if side == 0 else padded_row(BX)
            pot[0, face : face + BY, :] = zero

        @pl.when(jnp.logical_not(has["y" + way]))
        def _():
            for stage in range(STEPS):
                for s in range(SPECIES):
                    y_in[stage, side, s] = line
            recv[(LOW + side) * TILE : (LOW + side) * TILE + BX, :] = line

        @pl.when(jnp.logical_not(has["z" + way]))
        def _():
            for stage in range(STEPS):
                for s in range(SPECIES):
                    z_in[stage, side, s] = line

    for load in loads[:3]:
        load.wait()
    charge = cm[...].reshape(BX * PY, MODES)
    a, b = charge[:, : MODES // 2], charge[:, MODES // 2 :]
    dot = functools.partial(jnp.dot, preferred_element_type=F32)
    rims_of = []
    for turns in range(PZ):
        total = None
        for half, part in enumerate(quarter_turned(a, b, turns)):
            rows = slice(half * MODES // 2, (half + 1) * MODES // 2)
            part_high = part.astype(BF16)
            part_low = (part - part_high.astype(F32)).astype(BF16)
            term = dot(part_high, high[rows, :]) + (
                dot(part_low, high[rows, :]) + dot(part_high, low[rows, :])
            )
            total = term if total is None else total + term
        product[turns] = total
        turned = jnp.transpose(total)
        rims_of.append((turned[:1], turned[BZ - 1 :]))
        for q in range(PY):
            at = (turns * PY + q) * TILE
            tile = product[turns, pl.ds(q, BX, stride=PY), :]
            sendbuf[at : at + 1, :] = tile[:1]
            sendbuf[at + 1 : at + 2, :] = tile[BX - 1 :]
            sendbuf[at + 2 : at + BX, :] = tile[1 : BX - 1]
    nothing = jnp.zeros((1, BZ), F32)
    early = (lax.broadcasted_iota(jnp.int32, (1, BZ), 1) & (PY - 1)) < PY // 2
    for layer in range(PZ):
        below = rims_of[layer - 1][1] if layer > 0 else nothing
        above = rims_of[layer + 1][0] if layer < PZ - 1 else nothing
        above = pltpu.roll(above, PY // 2, 1)
        rows = (jnp.where(early, below, above), jnp.where(early, above, below))
        for q in range(PY):
            at = (layer * PY + q) * TILE + BX
            sendbuf[at : at + 1, :] = rows[q // (PY // 2)]

    pl.semaphore_wait(
        barrier,
        NYZ - 1 + has["x+"].astype(jnp.int32) + has["x-"].astype(jnp.int32),
    )

    def part(ref, index, start, count):
        return ref.at[pl.ds(index * TILE + start, count), :]

    def send_part(number, start, count):
        def act(peer):
            pltpu.make_async_remote_copy(
                src_ref=part(sendbuf, peer, start, count),
                dst_ref=part(recv, me, start, count),
                send_sem=a2a_send.at[number], recv_sem=a2a_recv.at[number],
                device_id={"yz": peer}, device_id_type=MESH,
            ).start()
        return act

    def bytes_of(ref, rows, sem):
        return pltpu.make_async_copy(ref.at[pl.ds(0, rows), :], ref.at[pl.ds(0, rows), :], sem)

    first, last = me == 0, me == NYZ - 1
    FACE_ROWS, REST_ROWS = (NYZ - 1) * FACE, (NYZ - 1) * (TILE - FACE)
    EDGE_ROWS = (PZ * (PY - 1) - 1) * BX

    def edge_copy(tile, peer, slot):
        return pltpu.make_async_remote_copy(
            src_ref=part(sendbuf, tile, 0, BX), dst_ref=part(recv, slot, 0, BX),
            send_sem=edge_send, recv_sem=edge_recv.at[slot - NYZ],
            device_id={"yz": peer}, device_id_type=MESH,
        )

    def send_rest(peer):
        send_part(1, FACE, TILE - FACE)(peer)
        q = lax.rem(peer, PY)
        pl.when(last & (q > 0))(lambda: edge_copy(peer - 1, peer, LOW).start())
        pl.when(first & (q < PY - 1))(lambda: edge_copy(peer + 1, peer, HIGH).start())

    partners(send_part(0, 0, FACE))

    def halo_copy(stage, way, fields):
        number = ways.index(way)
        side = 0 if way[1] == "+" else 1
        if way[0] == "x":
            src = fields.at[:, pl.ds(padded_row(BX - 1 if side == 0 else 0), BY), :]
            if stage == STEPS:
                dst = fields.at[:, pl.ds(TOP if side == 0 else padded_row(BX), BY), :]
            else:
                dst = x_in.at[stage, side]
        elif way[0] == "y":
            src, dst = y_out.at[stage, side], y_in.at[stage, side]
        else:
            src, dst = z_out.at[stage], z_in.at[stage, side]
        return pltpu.make_async_remote_copy(
            src_ref=src, dst_ref=dst,
            send_sem=halo_send.at[stage, number], recv_sem=halo_recv.at[stage, number],
            device_id=ids[way], device_id_type=MESH,
        )

    def start(stage, fields, which=ways):
        for way in which:
            pl.when(has[way])(lambda: halo_copy(stage, way, fields).start())

    def receive(stage, fields, which=ways):
        for way in which:
            pl.when(has[back[way]])(lambda: halo_copy(stage, way, fields).wait_recv())

    def finish(stage, fields, which=ways):
        for way in which:
            pl.when(has[way])(lambda: halo_copy(stage, way, fields).wait_send())

    def rims(stage, s, fields, planes=tuple(range(BX)), packed=None):
        for x in planes:
            plane = fields[s, padded_row(x) : padded_row(x) + BY, :]
            whole = pack_plane(plane, x)
            if packed is None:
                packed = whole
            else:
                packed = jnp.where((lanes() >= 16 * x - 1) & (lanes() < 16 * x + 15), whole, packed)
        return packed

    def finish_rims(stage, s, fields, packed):
        z_out[stage, s] = packed
        y_out[stage, 0, s] = fields[s, pl.ds(padded_row(0) + BY - 1, BX, stride=ROWS), :]
        y_out[stage, 1, s] = fields[s, pl.ds(padded_row(0), BX, stride=ROWS), :]

    def arrived_lanes(stage, s):
        even = (lanes() & 1) == 0
        below, above = z_in[stage, 0, s], z_in[stage, 1, s]
        return jnp.where(even, pltpu.roll(below, 1, 1), pltpu.roll(above, BZ - 1, 1))

    lane = lax.broadcasted_iota(jnp.int32, (BY, BZ), 1)
    at_low = lane == 0
    half_low, half_high = lane[:HALF] == 0, lane[:HALF] == BZ - 1

    def differences(fields, s, x, y):
        r = padded_row(x) + y
        centre = fields[s, r : r + HALF, :]
        x_plus, x_minus = fields[s, r + ROWS : r + ROWS + HALF, :], fields[s, r - ROWS : r - ROWS + HALF, :]
        y_plus, y_minus = fields[s, r + 1 : r + 1 + HALF, :], fields[s, r - 1 : r - 1 + HALF, :]
        z_plus = jnp.where(half_high, 0.0, pltpu.roll(centre, BZ - 1, 1))
        z_minus = jnp.where(half_low, 0.0, pltpu.roll(centre, 1, 1))
        spread = (x_plus + x_minus) + (y_plus + y_minus) + (z_plus + z_minus) - 6.0 * centre
        return centre, spread, (x_plus - x_minus, y_plus - y_minus, z_plus - z_minus)

    def quarter_valence(s):
        return jnp.where(s == 0, 0.25, jnp.where(s == 2, 0.5, -0.25)).astype(F32)

    for load in lam_loads:
        load.wait()

    @pl.loop(0, SPECIES)
    def _(s):
        finish_rims(0, s, l0, rims(0, s, l0))

    start(0, l0)
    partners(send_rest)
    mine = pl.ds(me * TILE, TILE)
    recv[mine, :] = sendbuf[mine, :]

    @pl.when(last)
    def _():
        recv[LOW * TILE : LOW * TILE + BX, :] = sendbuf[(NYZ - 2) * TILE : (NYZ - 2) * TILE + BX, :]

    @pl.when(first)
    def _():
        recv[HIGH * TILE : HIGH * TILE + BX, :] = sendbuf[TILE : TILE + BX, :]

    for load in loads[3:]:
        load.wait()

    @pl.loop(0, SPECIES)
    def _(s):
        charge_of = quarter_valence(s)
        for x in range(BX):
            for y in range(0, BY, HALF):
                rows = slice(x * BY + y, x * BY + y + HALF)
                centre, spread, diff = differences(l0, s, x, y)
                diffusion = dif[s, rows, :]
                scaled = charge_of * diffusion
                total = centre + diffusion * spread
                for axis in range(3):
                    total = total + (0.5 * vel[axis, rows, :]) * diff[axis]
                    grad[axis, s, rows, :] = scaled * diff[axis]
                base[s, rows, :] = total

    bytes_of(recv, FACE_ROWS, a2a_recv.at[0]).wait()

    def assemble(x):
        pot[0, padded_row(x) : padded_row(x) + BY, :] = recv[pl.ds(PLACE[x], BY, stride=TILE), :]

    assemble(0)
    assemble(BX - 1)
    start(STEPS, pot, ("x+", "x-"))

    def rim_terms(axis, side, s, rows):
        diffusion, flow = dif[s, rows, :], 0.5 * vel[axis, rows, :]
        scaled = quarter_valence(s) * diffusion
        if side == 0:
            return diffusion - flow, -scaled
        return diffusion + flow, scaled

    receive(0, l0)

    @pl.loop(0, SPECIES)
    def _(s):
        for side in (0, 1):
            x = (BX - 1) * side
            rows = slice(x * BY, (x + 1) * BY)
            value = x_in[0, side, s]
            to_base, to_grad = rim_terms(0, side, s, rows)
            base[s, rows, :] += to_base * value
            grad[0, s, rows, :] += to_grad * value
            rows = pl.ds((BY - 1) * side, BX, stride=BY)
            value = y_in[0, side, s]
            to_base, to_grad = rim_terms(1, side, s, rows)
            base[s, rows, :] += to_base * value
            grad[1, s, rows, :] += to_grad * value
        packed = arrived_lanes(0, s)
        for x in range(BX):
            rows = slice(x * BY, (x + 1) * BY)
            value = unpack_plane(packed, x)
            diffusion, flow = dif[s, rows, :], 0.5 * vel[2, rows, :]
            scaled = quarter_valence(s) * diffusion
            base[s, rows, :] += (diffusion + jnp.where(at_low, -flow, flow)) * value
            grad[2, s, rows, :] += jnp.where(at_low, -scaled, scaled) * value

    bytes_of(recv, REST_ROWS, a2a_recv.at[1]).wait()
    pl.when(has["y-"] & jnp.logical_not(last))(lambda: edge_copy(0, lax.rem(me + 1, NYZ), LOW).wait_recv())
    pl.when(has["y+"] & jnp.logical_not(first))(lambda: edge_copy(0, lax.rem(me + 1, NYZ), HIGH).wait_recv())
    for x in range(1, BX - 1):
        assemble(x)
    for x in range(BX):
        for side, row in ((0, padded_row(x) - 1), (1, padded_row(x) + BY)):
            at = (LOW + side) * TILE + PLACE[x]
            pot[0, row : row + 1, :] = recv[at : at + 1, :]
    z_rims = pltpu.roll(recv[pl.ds(BX, BY, stride=TILE), :], lax.rem(BZ - p, BZ), 1)

    def slopes(x):
        r = padded_row(x)
        rows = slice(x * BY, (x + 1) * BY)
        centre = pot[0, r : r + BY, :]
        low_rim = pltpu.roll(z_rims, (BZ - 16 * x) % BZ, 1) if x else z_rims
        high_rim = pltpu.roll(z_rims, (2 * BZ - 1 - 16 * x - 8) % BZ, 1)
        z_plus = jnp.where(lane == BZ - 1, high_rim, pltpu.roll(centre, BZ - 1, 1))
        z_minus = jnp.where(at_low, low_rim, pltpu.roll(centre, 1, 1))
        slope[0, rows, :] = pot[0, r + ROWS : r + ROWS + BY, :] - pot[0, r - ROWS : r - ROWS + BY, :]
        slope[1, rows, :] = pot[0, r + 1 : r + 1 + BY, :] - pot[0, r - 1 : r - 1 + BY, :]
        slope[2, rows, :] = z_plus - z_minus

    def first_step(s, x):
        rows = slice(x * BY, (x + 1) * BY)
        total = base[s, rows, :]
        for axis in range(3):
            total = total - slope[axis, rows, :] * grad[axis, s, rows, :]
        l1[s, padded_row(x) : padded_row(x) + BY, :] = total

    inner = tuple(range(1, BX - 1))
    for x in inner:
        slopes(x)

    @pl.loop(0, SPECIES)
    def _(s):
        for x in inner:
            first_step(s, x)
        z_out[1, s] = rims(1, s, l1, inner, line)

    receive(STEPS, pot, ("x+", "x-"))
    for x in (0, BX - 1):
        slopes(x)

    @pl.loop(0, SPECIES)
    def _(s):
        for x in (0, BX - 1):
            first_step(s, x)
        outer = rims(1, s, l1, (0, BX - 1))
        own = (lanes() >= 15) & (lanes() < 111)
        finish_rims(1, s, l1, jnp.where(own, z_out[1, s], outer))

    start(1, l1)

    def own_values(step, now, later, row_of):
        @pl.loop(0, SPECIES)
        def _(s):
            charge_of = quarter_valence(s)
            for x in range(BX):
                for y in range(0, BY, HALF):
                    rows = slice(x * BY + y, x * BY + y + HALF)
                    centre, spread, diff = differences(now, s, x, y)
                    diffusion = dif[s, rows, :]
                    total = centre + diffusion * spread
                    scaled = charge_of * diffusion
                    for axis in range(3):
                        if step == 1:
                            rate = 0.5 * vel[axis, rows, :] - scaled * slope[axis, rows, :]
                            along[axis, s, rows, :] = rate
                        else:
                            rate = along[axis, s, rows, :]
                        total = total + rate * diff[axis]
                    r = row_of(x) + y
                    later[s, r : r + HALF, :] = total

    def rim_values(step, later, row_of, after):
        @pl.loop(0, SPECIES)
        def _(s):
            apart = row_of(1) - row_of(0)
            for side in (0, 1):
                x = (BX - 1) * side
                rows = slice(x * BY, (x + 1) * BY)
                rate = along[0, s, rows, :]
                factor = dif[s, rows, :] + (rate if side else -rate)
                later[s, row_of(x) : row_of(x) + BY, :] += factor * x_in[step, side, s]
                rows = pl.ds((BY - 1) * side, BX, stride=BY)
                rate = along[1, s, rows, :]
                factor = dif[s, rows, :] + (rate if side else -rate)
                later[s, pl.ds(row_of(0) + (BY - 1) * side, BX, stride=apart), :] += factor * y_in[step, side, s]
            packed = arrived_lanes(step, s)
            for x in range(BX):
                rows = slice(x * BY, (x + 1) * BY)
                rate = along[2, s, rows, :]
                factor = dif[s, rows, :] + jnp.where(at_low, -rate, rate)
                later[s, row_of(x) : row_of(x) + BY, :] += factor * unpack_plane(packed, x)
            after(s)

    own_values(1, l1, l2, padded_row)
    receive(1, l1)
    rim_values(1, l2, padded_row, lambda s: finish_rims(2, s, l2, rims(2, s, l2)))
    start(2, l2)

    flat_row = lambda x: x * BY
    own_values(2, l2, l3, flat_row)
    receive(2, l2)
    rim_values(
        2, l3, flat_row,
        lambda s: None,
    )

    bytes_of(sendbuf, FACE_ROWS, a2a_send.at[0]).wait()
    bytes_of(sendbuf, REST_ROWS, a2a_send.at[1]).wait()
    pl.when(first | last)(lambda: bytes_of(sendbuf, EDGE_ROWS, edge_send).wait())
    for stage, ref in enumerate((l0, l1, l2)):
        finish(stage, ref)
    finish(STEPS, pot, ("x+", "x-"))


def hand_over_kernel(source, target, sems):
    copies = [
        pltpu.make_async_copy(source.at[s], target.at[s], sems.at[s]) for s in range(SPECIES)
    ]
    for copy in copies:
        copy.start()
    for copy in copies:
        copy.wait()


def body(terminal_adjoint, diffusivity, velocity, charge_modes):
    high, low = base_table()
    cells = BX * BY
    brick = (SPECIES, cells, BZ)
    padded = (SPECIES, (BX + 2) * ROWS, BZ)
    flow = (3, cells, BZ)
    anywhere = pl.BlockSpec(memory_space=pl.ANY)
    out = pl.pallas_call(
        slab_kernel,
        out_shape=pltpu.VMEM(brick, F32),
        in_specs=[anywhere] * 6,
        out_specs=pl.BlockSpec(memory_space=pltpu.VMEM),
        scratch_shapes=[
            pltpu.VMEM(padded, F32), pltpu.VMEM(padded, F32), pltpu.VMEM(padded, F32),
            pltpu.VMEM(brick, F32),
            pltpu.VMEM(flow, F32),
            pltpu.VMEM((3,) + brick, F32),
            pltpu.VMEM(brick, F32),
            pltpu.VMEM((3,) + brick, F32),
            pltpu.VMEM(flow, F32),
            pltpu.VMEM((1,) + padded[1:], F32),
            pltpu.VMEM((BX, PY, MODES), F32),
            pltpu.VMEM((MODES, BZ), BF16), pltpu.VMEM((MODES, BZ), BF16),
            pltpu.VMEM((PZ, BX * PY, BZ), F32),
            pltpu.VMEM((NYZ * TILE, BZ), F32),
            pltpu.VMEM(((NYZ + 2) * TILE, BZ), F32),
            pltpu.VMEM((STEPS, 2, SPECIES, BY, BZ), F32),
            pltpu.VMEM((STEPS, 2, SPECIES, BX, BZ), F32),
            pltpu.VMEM((STEPS, 2, SPECIES, BX, BZ), F32),
            pltpu.VMEM((STEPS, SPECIES, 8, BZ), F32),
            pltpu.VMEM((STEPS, 2, SPECIES, 8, BZ), F32),
            pltpu.SemaphoreType.DMA((5,)),
            pltpu.SemaphoreType.DMA((BX,)),
            pltpu.SemaphoreType.DMA((SPECIES,)),
            pltpu.SemaphoreType.DMA((2,)),
            pltpu.SemaphoreType.DMA((2,)),
            pltpu.SemaphoreType.DMA,
            pltpu.SemaphoreType.DMA((2,)),
            pltpu.SemaphoreType.DMA((STEPS + 1, 6)),
            pltpu.SemaphoreType.DMA((STEPS + 1, 6)),
        ],
        compiler_params=pltpu.CompilerParams(
            collective_id=0, has_side_effects=True, vmem_limit_bytes=60 * 1024 * 1024
        ),
    )(
        terminal_adjoint.reshape(SPECIES, BX, BY, BZ),
        diffusivity.reshape(brick),
        velocity.reshape(flow),
        charge_modes.reshape(BX, PY, MODES),
        jnp.asarray(high),
        jnp.asarray(low),
    )
    return out.reshape(terminal_adjoint.shape)


def solution(mesh):
    return jax.shard_map(
        body,
        mesh=mesh,
        in_specs=(
            P(None, "gx", None, "yz", None),
            P(None, "gx", None, "yz", None),
            P(None, "gx", None, "yz", None),
            P("gx", "yz", None, None),
        ),
        out_specs=P(None, "gx", None, "yz", None),
        check_vma=False,
    )
```

```python
import functools
import math

import jax
import jax.numpy as jnp
import ml_dtypes
import numpy as np
from jax import lax
from jax.experimental import pallas as pl
from jax.experimental.pallas import tpu as pltpu
from jax.sharding import PartitionSpec as P

SPECIES = 4
STEPS = 3
SCREEN = 1.0
MESH = pl.DeviceIdType.MESH

PZ, PY = 4, 16
NYZ = PZ * PY
BX, BY, BZ = 8, 64, 128
MODES = 512
TOP, ROWS = 8, 80
TILE = BX + 1
PLACE = {x: (x + 1) % BX for x in range(BX)}
FACE = 2
LOW, HIGH = NYZ, NYZ + 1
HALF = 32
F32, BF16 = jnp.float32, jnp.bfloat16


def base_table():
    half = MODES // 2
    modes = np.arange(half)[:, None]
    cells = np.arange(BZ)[None, :]
    angle = (modes * cells % MODES) * (2.0 * math.pi / MODES)
    theta = modes * (2.0 * math.pi / MODES)
    green = 1.0 / (1.0 + SCREEN * theta * theta)
    table = np.concatenate([np.cos(angle) * green, np.sin(angle) * green], 0)
    high = table.astype(np.float32).astype(ml_dtypes.bfloat16)
    low = (table - high.astype(np.float64)).astype(ml_dtypes.bfloat16)
    return high, low


def quarter_turned(a, b, turns):
    if turns == 0:
        return a, b
    k = lax.broadcasted_iota(jnp.int32, a.shape, 1)
    odd = (k & 1) == 1
    if turns == 2:
        return jnp.where(odd, -a, a), jnp.where(odd, -b, b)
    third = (k & 2) == 2
    if turns == 3:
        third = third != odd
    cos_part = jnp.where(odd, b, a)
    sin_part = jnp.where(odd, a, b)
    cos_part = jnp.where(third, -cos_part, cos_part)
    sin_part = jnp.where(third != odd, -sin_part, sin_part)
    return cos_part, sin_part


def lanes():
    return lax.broadcasted_iota(jnp.int32, (8, BZ), 1)


def pack_plane(plane, x):
    lane = lanes()
    parts = [plane[8 * r : 8 * r + 8] for r in range(8)]
    width = 2
    while len(parts) > 1:
        moved = (lane >= width - 1) & (lane < 2 * width - 1)
        parts = [
            jnp.where(moved, pltpu.roll(right, width, 1), left)
            for left, right in zip(parts[::2], parts[1::2])
        ]
        width *= 2
    whole = parts[0]
    if x > 0:
        whole = pltpu.roll(whole, 16 * x, 1)
    return whole


def merged(packed, whole, x):
    lane = lanes()
    if x == 0:
        return whole
    return jnp.where((lane >= 16 * x - 1) & (lane < 16 * x + 15), whole, packed)


def unpack_plane(packed, x):
    lane = lanes()
    rim = (lane == 0) | (lane == BZ - 1)
    shifts = [(BZ - 16 * x - 2 * r) % BZ for r in range(8)]
    moved = [pltpu.roll(packed, shift, 1) if shift else packed for shift in shifts]
    return jnp.concatenate([jnp.where(rim, part, 0.0) for part in moved], 0)


def padded_row(x):
    return (x + 1) * ROWS + TOP


def slab_kernel(
    lam_hbm, dif_hbm, vel_hbm, cm_hbm, high_hbm, low_hbm, l3,
    l0, l1, l2, dif, vel, along, base, grad, slope, pot, cm, high, low,
    product, sendbuf, recv, x_in, y_out, y_in, z_out, z_in, packs, factors, came,
    load_sem, lam_sem, a2a_send, a2a_recv, edge_send, edge_recv, pass_send, pass_recv, halo_send, halo_recv,
):
    gx = lax.axis_index("gx")
    me = lax.axis_index("yz")
    ngx = lax.axis_size("gx")
    p = me & (PY - 1)
    zb = me >> 4
    mx, mz, my = me & 3, (me >> 2) & 7, me >> 5
    has = {
        "x+": gx < ngx - 1, "x-": gx > 0,
        "y+": p < PY - 1, "y-": p > 0,
        "z+": zb < PZ - 1, "z-": zb > 0,
    }
    ids = {
        "x+": {"gx": gx + 1}, "x-": {"gx": gx - 1},
        "y+": {"yz": me + 1}, "y-": {"yz": me - 1},
        "z+": {"yz": me + PY}, "z-": {"yz": me - PY},
    }
    ways = ("z+", "z-", "x+", "x-", "y+", "y-")
    back = {"x+": "x-", "x-": "x+", "y+": "y-", "y-": "y+", "z+": "z-", "z-": "z+"}

    def partners(act):
        @pl.loop(0, 8)
        def _(j):
            step = (j + 1) >> 1
            z = (mz + 4 + jnp.where((j & 1) == 0, -step, step)) & 7
            for dx in (2, 1, 3, 0):
                for dy in (1, 0):
                    x = (mx + dx) & 3
                    y = 1 - my if dy else my
                    peer = (y * 8 + z) * 4 + x
                    if dx or dy:
                        act(peer)
                    else:
                        pl.when(j < 7)(functools.partial(act, peer))

    barrier = pltpu.get_barrier_semaphore()
    partners(
        lambda peer: pl.semaphore_signal(
            barrier, inc=1, device_id={"yz": peer}, device_id_type=MESH
        )
    )
    for way in ("x+", "x-"):
        @pl.when(has[way])
        def _():
            pl.semaphore_signal(barrier, inc=1, device_id=ids[way], device_id_type=MESH)

    loads = [
        pltpu.make_async_copy(cm_hbm, cm, load_sem.at[0]),
        pltpu.make_async_copy(high_hbm, high, load_sem.at[1]),
        pltpu.make_async_copy(low_hbm, low, load_sem.at[2]),
        pltpu.make_async_copy(dif_hbm, dif, load_sem.at[3]),
        pltpu.make_async_copy(vel_hbm, vel, load_sem.at[4]),
    ]
    lam_loads = [
        pltpu.make_async_copy(lam_hbm.at[:, x], l0.at[:, pl.ds(padded_row(x), BY), :], lam_sem.at[x])
        for x in range(BX)
    ]
    for load in loads[:3] + lam_loads + loads[3:]:
        load.start()

    zero = jnp.zeros((BY, BZ), F32)
    line = jnp.zeros((BX, BZ), F32)
    for ref in (l0, l1, l2):
        @pl.loop(0, SPECIES)
        def _(s):
            ref[s, TOP : TOP + BY, :] = zero
            ref[s, padded_row(BX) : padded_row(BX) + BY, :] = zero
            ref[s, pl.ds(padded_row(0) - 1, BX, stride=ROWS), :] = line
            ref[s, pl.ds(padded_row(0) + BY, BX, stride=ROWS), :] = line

    for side, way in enumerate(("-", "+")):
        @pl.when(jnp.logical_not(has["x" + way]))
        def _():
            for stage in range(STEPS):
                for s in range(SPECIES):
                    x_in[stage, side, s] = zero
            face = TOP if side == 0 else padded_row(BX)
            pot[0, face : face + BY, :] = zero

        @pl.when(jnp.logical_not(has["y" + way]))
        def _():
            for stage in range(STEPS):
                for s in range(SPECIES):
                    y_in[stage, side, s] = line
            recv[(LOW + side) * TILE : (LOW + side) * TILE + BX, :] = line

        @pl.when(jnp.logical_not(has["z" + way]))
        def _():
            for stage in range(STEPS):
                for pair in range(SPECIES // 2):
                    z_in[stage, side, pair] = line

    for load in loads[:3]:
        load.wait()
    charge = cm[...].reshape(BX * PY, MODES)
    a, b = charge[:, : MODES // 2], charge[:, MODES // 2 :]
    dot = functools.partial(jnp.dot, preferred_element_type=F32)
    rims_of = []
    for turns in range(PZ):
        total = None
        for half, part in enumerate(quarter_turned(a, b, turns)):
            rows = slice(half * MODES // 2, (half + 1) * MODES // 2)
            part_high = part.astype(BF16)
            part_low = (part - part_high.astype(F32)).astype(BF16)
            term = dot(part_high, high[rows, :]) + (
                dot(part_low, high[rows, :]) + dot(part_high, low[rows, :])
            )
            total = term if total is None else total + term
        product[turns] = total
        turned = jnp.transpose(total)
        rims_of.append((turned[:1], turned[BZ - 1 :]))
        for q in range(PY):
            at = (turns * PY + q) * TILE
            sendbuf[pl.ds(at, BX), :] = pltpu.roll(product[turns, pl.ds(q, BX, stride=PY), :], 1, 0)
    nothing = jnp.zeros((1, BZ), F32)
    odd = (lax.broadcasted_iota(jnp.int32, (1, BZ), 1) & 1) == 1
    for layer in range(PZ):
        below = rims_of[layer - 1][1] if layer > 0 else nothing
        above = rims_of[layer + 1][0] if layer < PZ - 1 else nothing
        above = pltpu.roll(above, BZ - 1, 1)
        rows = (jnp.where(odd, above, below), jnp.where(odd, below, above))
        for q in range(PY):
            at = (layer * PY + q) * TILE + BX
            sendbuf[at : at + 1, :] = rows[q % 2]

    pl.semaphore_wait(
        barrier,
        NYZ - 1 + has["x+"].astype(jnp.int32) + has["x-"].astype(jnp.int32),
    )

    def part(ref, index, start, count):
        return ref.at[pl.ds(index * TILE + start, count), :]

    def send_part(number, start, count):
        def act(peer):
            pltpu.make_async_remote_copy(
                src_ref=part(sendbuf, peer, start, count),
                dst_ref=part(recv, me, start, count),
                send_sem=a2a_send.at[number], recv_sem=a2a_recv.at[number],
                device_id={"yz": peer}, device_id_type=MESH,
            ).start()
        return act

    def bytes_of(ref, rows, sem):
        return pltpu.make_async_copy(ref.at[pl.ds(0, rows), :], ref.at[pl.ds(0, rows), :], sem)

    first, last = me == 0, me == NYZ - 1
    special = first | last

    def edge_tile(peer, side):
        return pltpu.make_async_remote_copy(
            src_ref=part(sendbuf, peer, 0, TILE), dst_ref=part(recv, me, 0, TILE),
            send_sem=edge_send, recv_sem=edge_recv.at[side],
            device_id={"yz": peer}, device_id_type=MESH,
        )

    def pass_on(side):
        return pltpu.make_async_remote_copy(
            src_ref=part(recv, (NYZ - 1) * (1 - side), 0, BX), dst_ref=part(recv, LOW + side, 0, BX),
            send_sem=pass_send.at[side], recv_sem=pass_recv.at[side],
            device_id=ids["y-" if side else "y+"], device_id_type=MESH,
        )

    mine = pl.ds(me * TILE, TILE)
    recv[mine, :] = sendbuf[mine, :]
    pl.when(last)(lambda: partners(lambda peer: edge_tile(peer, 0).start()))
    pl.when(first)(lambda: partners(lambda peer: edge_tile(peer, 1).start()))
    pl.when(jnp.logical_not(special))(lambda: partners(send_part(0, 0, FACE)))

    def arrived(number, rows):
        pl.when(special)(lambda: bytes_of(recv, (NYZ - 2) * rows, a2a_recv.at[number]).wait())
        pl.when(jnp.logical_not(special))(
            lambda: bytes_of(recv, (NYZ - 3) * rows, a2a_recv.at[number]).wait()
        )

    def halo_copy(stage, way, fields):
        number = ways.index(way)
        side = 0 if way[1] == "+" else 1
        if way[0] == "x":
            src = fields.at[:, pl.ds(padded_row(BX - 1 if side == 0 else 0), BY), :]
            if stage == STEPS:
                dst = fields.at[:, pl.ds(TOP if side == 0 else padded_row(BX), BY), :]
            else:
                dst = x_in.at[stage, side]
        elif way[0] == "y":
            src, dst = y_out.at[stage, side], y_in.at[stage, side]
        else:
            src, dst = z_out.at[stage, side], z_in.at[stage, side]
        return pltpu.make_async_remote_copy(
            src_ref=src, dst_ref=dst,
            send_sem=halo_send.at[stage, number], recv_sem=halo_recv.at[stage, number],
            device_id=ids[way], device_id_type=MESH,
        )

    def start(stage, fields, which=ways):
        for way in which:
            pl.when(has[way])(lambda: halo_copy(stage, way, fields).start())

    def receive(stage, fields, which=ways):
        for way in which:
            pl.when(has[back[way]])(lambda: halo_copy(stage, way, fields).wait_recv())

    def finish(stage, fields, which=ways):
        for way in which:
            pl.when(has[way])(lambda: halo_copy(stage, way, fields).wait_send())

    def merge(packed, plane, x):
        whole = pack_plane(plane, x)
        if packed is None:
            return whole
        return jnp.where(((lanes() + 1 - 16 * x) & (BZ - 1)) < 16, whole, packed)

    def packed_rims(plane_of):
        packed = None
        for x in range(BX):
            packed = merge(packed, plane_of(x), x)
        return packed

    even = (lanes() & 1) == 0

    def send_lanes(stage, fields, packed):
        for pair in range(SPECIES // 2):
            one, two = packed(2 * pair), packed(2 * pair + 1)
            z_out[stage, 0, pair] = jnp.where(even, pltpu.roll(two, 1, 1), one)
            z_out[stage, 1, pair] = jnp.where(even, one, pltpu.roll(two, BZ - 1, 1))
        start(stage, fields, ("z+", "z-"))

    def receive_lanes(stage, fields):
        receive(stage, fields, ("z+", "z-"))
        for pair in range(SPECIES // 2):
            below, above = z_in[stage, 0, pair], z_in[stage, 1, pair]
            came[2 * pair] = jnp.where(even, pltpu.roll(below, 1, 1), pltpu.roll(above, BZ - 1, 1))
            came[2 * pair + 1] = jnp.where(even, below, above)

    def send_rows(stage, fields):
        for s in range(SPECIES):
            y_out[stage, 0, s] = fields[s, pl.ds(padded_row(0) + BY - 1, BX, stride=ROWS), :]
            y_out[stage, 1, s] = fields[s, pl.ds(padded_row(0), BX, stride=ROWS), :]
        start(stage, fields, ("y+", "y-"))

    def own_plane(fields, s, x):
        return fields[s, padded_row(x) : padded_row(x) + BY, :]

    lane = lax.broadcasted_iota(jnp.int32, (BY, BZ), 1)
    at_low = lane == 0
    half_low, half_high = lane[:HALF] == 0, lane[:HALF] == BZ - 1

    def differences(fields, s, x, y):
        r = padded_row(x) + y
        centre = fields[s, r : r + HALF, :]
        x_plus, x_minus = fields[s, r + ROWS : r + ROWS + HALF, :], fields[s, r - ROWS : r - ROWS + HALF, :]
        y_plus, y_minus = fields[s, r + 1 : r + 1 + HALF, :], fields[s, r - 1 : r - 1 + HALF, :]
        z_plus = jnp.where(half_high, 0.0, pltpu.roll(centre, BZ - 1, 1))
        z_minus = jnp.where(half_low, 0.0, pltpu.roll(centre, 1, 1))
        spread = (x_plus + x_minus) + (y_plus + y_minus) + (z_plus + z_minus) - 6.0 * centre
        return centre, spread, (x_plus - x_minus, y_plus - y_minus, z_plus - z_minus)

    def quarter_valence(s):
        return jnp.where(s == 0, 0.25, jnp.where(s == 2, 0.5, -0.25)).astype(F32)

    for load in lam_loads:
        load.wait()

    @pl.loop(0, SPECIES)
    def _(s):
        packs[s] = packed_rims(lambda x: own_plane(l0, s, x))

    send_lanes(0, l0, lambda s: packs[s])
    start(0, l0, ("x+", "x-"))
    send_rows(0, l0)
    pl.when(jnp.logical_not(special))(lambda: partners(send_part(1, FACE, TILE - FACE)))

    for load in loads[3:]:
        load.wait()

    @pl.loop(0, SPECIES)
    def _(s):
        charge_of = quarter_valence(s)
        for x in range(BX):
            for y in range(0, BY, HALF):
                rows = slice(x * BY + y, x * BY + y + HALF)
                centre, spread, diff = differences(l0, s, x, y)
                diffusion = dif[s, rows, :]
                scaled = charge_of * diffusion
                total = centre + diffusion * spread
                for axis in range(3):
                    total = total + (0.5 * vel[axis, rows, :]) * diff[axis]
                    grad[axis, s, rows, :] = scaled * diff[axis]
                base[s, rows, :] = total

    pl.when(jnp.logical_not(last))(lambda: edge_tile(lax.rem(me + 1, NYZ), 0).wait_recv())
    pl.when(jnp.logical_not(first))(lambda: edge_tile(lax.rem(me + 1, NYZ), 1).wait_recv())
    pl.when(has["y+"])(lambda: pass_on(0).start())
    pl.when(has["y-"])(lambda: pass_on(1).start())
    arrived(0, FACE)

    def assemble(x):
        pot[0, padded_row(x) : padded_row(x) + BY, :] = recv[pl.ds(PLACE[x], BY, stride=TILE), :]

    assemble(0)
    assemble(BX - 1)
    start(STEPS, pot, ("x+", "x-"))

    def rim_terms(axis, side, s, rows):
        diffusion, flow = dif[s, rows, :], 0.5 * vel[axis, rows, :]
        scaled = quarter_valence(s) * diffusion
        if side == 0:
            return diffusion - flow, -scaled
        return diffusion + flow, scaled

    receive(0, l0, ("x+", "x-", "y+", "y-"))
    receive_lanes(0, l0)

    @pl.loop(0, SPECIES)
    def _(s):
        for side in (0, 1):
            x = (BX - 1) * side
            rows = slice(x * BY, (x + 1) * BY)
            value = x_in[0, side, s]
            to_base, to_grad = rim_terms(0, side, s, rows)
            base[s, rows, :] += to_base * value
            grad[0, s, rows, :] += to_grad * value
            rows = pl.ds((BY - 1) * side, BX, stride=BY)
            value = y_in[0, side, s]
            to_base, to_grad = rim_terms(1, side, s, rows)
            base[s, rows, :] += to_base * value
            grad[1, s, rows, :] += to_grad * value
        for x in range(BX):
            rows = slice(x * BY, (x + 1) * BY)
            value = unpack_plane(came[s], x)
            diffusion, flow = dif[s, rows, :], 0.5 * vel[2, rows, :]
            scaled = quarter_valence(s) * diffusion
            base[s, rows, :] += (diffusion + jnp.where(at_low, -flow, flow)) * value
            grad[2, s, rows, :] += jnp.where(at_low, -scaled, scaled) * value

    arrived(1, TILE - FACE)
    for x in range(1, BX - 1):
        assemble(x)
    pl.when(has["y-"])(lambda: pass_on(0).wait_recv())
    pl.when(has["y+"])(lambda: pass_on(1).wait_recv())
    for side, row in ((0, padded_row(0) - 1), (1, padded_row(0) + BY)):
        at = (LOW + side) * TILE
        pot[0, pl.ds(row, BX - 1, stride=ROWS), :] = recv[at + 1 : at + BX, :]
        row += (BX - 1) * ROWS
        pot[0, row : row + 1, :] = recv[at : at + 1, :]
    z_rims = pltpu.roll(recv[pl.ds(BX, BY, stride=TILE), :], (BZ - p) & (BZ - 1), 1)

    def first_step(x, packed):
        rims_here = pltpu.roll(z_rims, BZ - 16 * x, 1) if x else z_rims
        for y in range(0, BY, HALF):
            r = padded_row(x) + y
            rows = slice(x * BY + y, x * BY + y + HALF)
            centre = pot[0, r : r + HALF, :]
            rim = rims_here[y : y + HALF]
            z_plus = jnp.where(half_high, rim, pltpu.roll(centre, BZ - 1, 1))
            z_minus = jnp.where(half_low, rim, pltpu.roll(centre, 1, 1))
            here = (
                pot[0, r + ROWS : r + ROWS + HALF, :] - pot[0, r - ROWS : r - ROWS + HALF, :],
                pot[0, r + 1 : r + 1 + HALF, :] - pot[0, r - 1 : r - 1 + HALF, :],
                z_plus - z_minus,
            )
            for axis in range(3):
                slope[axis, rows, :] = here[axis]
            for s in range(SPECIES):
                total = base[s, rows, :]
                for axis in range(3):
                    total = total - here[axis] * grad[axis, s, rows, :]
                l1[s, r : r + HALF, :] = total
        return [merge(packed[s], own_plane(l1, s, x), x) for s in range(SPECIES)]

    packed = [line] * SPECIES
    for x in range(1, BX - 1):
        packed = first_step(x, packed)
    receive(STEPS, pot, ("x+", "x-"))
    for x in (0, BX - 1):
        packed = first_step(x, packed)
    send_lanes(1, l1, lambda s: packed[s])
    start(1, l1, ("x+", "x-"))
    send_rows(1, l1)

    def own_values(step, now, later, row_of):
        @pl.loop(0, SPECIES)
        def _(s):
            charge_of = quarter_valence(s)
            for x in range(BX):
                for y in range(0, BY, HALF):
                    rows = slice(x * BY + y, x * BY + y + HALF)
                    centre, spread, diff = differences(now, s, x, y)
                    diffusion = dif[s, rows, :]
                    total = centre + diffusion * spread
                    scaled = charge_of * diffusion
                    for axis in range(3):
                        if step == 1:
                            rate = 0.5 * vel[axis, rows, :] - scaled * slope[axis, rows, :]
                            along[axis, s, rows, :] = rate
                        else:
                            rate = along[axis, s, rows, :]
                        total = total + rate * diff[axis]
                    r = row_of(x) + y
                    later[s, r : r + HALF, :] = total

    def outer_values(step, later, row_of):
        apart = row_of(1) - row_of(0)

        @pl.loop(0, SPECIES)
        def _(s):
            for side in (0, 1):
                x = (BX - 1) * side
                rows = slice(x * BY, (x + 1) * BY)
                rate = along[0, s, rows, :]
                factor = dif[s, rows, :] + (rate if side else -rate)
                later[s, row_of(x) : row_of(x) + BY, :] += factor * x_in[step, side, s]
                rows = pl.ds((BY - 1) * side, BX, stride=BY)
                rate = along[1, s, rows, :]
                factor = dif[s, rows, :] + (rate if side else -rate)
                later[s, pl.ds(row_of(0) + (BY - 1) * side, BX, stride=apart), :] += factor * y_in[step, side, s]

    def lane_factor(s, x):
        rows = slice(x * BY, (x + 1) * BY)
        rate = along[2, s, rows, :]
        return dif[s, rows, :] + jnp.where(at_low, -rate, rate)

    def lane_values(s, planes, later, row_of):
        for x in planes:
            later[s, row_of(x) : row_of(x) + BY, :] += lane_factor(s, x) * unpack_plane(came[s], x)

    own_values(1, l1, l2, padded_row)

    @pl.loop(0, SPECIES)
    def _(s):
        factors[s] = packed_rims(lambda x: lane_factor(s, x))

    receive(1, l1, ("y+", "y-", "x+", "x-"))
    outer_values(1, l2, padded_row)

    @pl.loop(0, SPECIES)
    def _(s):
        packs[s] = packed_rims(lambda x: own_plane(l2, s, x))

    receive_lanes(1, l1)
    send_lanes(2, l2, lambda s: packs[s] + factors[s] * came[s])

    @pl.loop(0, SPECIES)
    def _(s):
        lane_values(s, (0, BX - 1), l2, padded_row)

    start(2, l2, ("x+", "x-"))

    @pl.loop(0, SPECIES)
    def _(s):
        lane_values(s, range(1, BX - 1), l2, padded_row)

    send_rows(2, l2)

    flat_row = lambda x: x * BY
    own_values(2, l2, l3, flat_row)
    receive(2, l2, ("y+", "y-", "x+", "x-"))
    outer_values(2, l3, flat_row)
    receive_lanes(2, l2)

    @pl.loop(0, SPECIES)
    def _(s):
        lane_values(s, range(BX), l3, flat_row)

    @pl.when(special)
    def _():
        bytes_of(sendbuf, (NYZ - 1) * TILE, edge_send).wait()

    @pl.when(jnp.logical_not(special))
    def _():
        bytes_of(sendbuf, (NYZ - 1) * FACE, a2a_send.at[0]).wait()
        bytes_of(sendbuf, (NYZ - 1) * (TILE - FACE), a2a_send.at[1]).wait()

    pl.when(has["y+"])(lambda: pass_on(0).wait_send())
    pl.when(has["y-"])(lambda: pass_on(1).wait_send())
    for stage, ref in enumerate((l0, l1, l2)):
        finish(stage, ref)
    finish(STEPS, pot, ("x+", "x-"))


def hand_over_kernel(source, target, sems):
    copies = [
        pltpu.make_async_copy(source.at[s], target.at[s], sems.at[s]) for s in range(SPECIES)
    ]
    for copy in copies:
        copy.start()
    for copy in copies:
        copy.wait()


def body(terminal_adjoint, diffusivity, velocity, charge_modes):
    high, low = base_table()
    cells = BX * BY
    brick = (SPECIES, cells, BZ)
    padded = (SPECIES, (BX + 2) * ROWS, BZ)
    flow = (3, cells, BZ)
    anywhere = pl.BlockSpec(memory_space=pl.ANY)
    out = pl.pallas_call(
        slab_kernel,
        out_shape=pltpu.VMEM(brick, F32),
        in_specs=[anywhere] * 6,
        out_specs=pl.BlockSpec(memory_space=pltpu.VMEM),
        scratch_shapes=[
            pltpu.VMEM(padded, F32), pltpu.VMEM(padded, F32), pltpu.VMEM(padded, F32),
            pltpu.VMEM(brick, F32),
            pltpu.VMEM(flow, F32),
            pltpu.VMEM((3,) + brick, F32),
            pltpu.VMEM(brick, F32),
            pltpu.VMEM((3,) + brick, F32),
            pltpu.VMEM(flow, F32),
            pltpu.VMEM((1,) + padded[1:], F32),
            pltpu.VMEM((BX, PY, MODES), F32),
            pltpu.VMEM((MODES, BZ), BF16), pltpu.VMEM((MODES, BZ), BF16),
            pltpu.VMEM((PZ, BX * PY, BZ), F32),
            pltpu.VMEM((NYZ * TILE, BZ), F32),
            pltpu.VMEM(((NYZ + 2) * TILE, BZ), F32),
            pltpu.VMEM((STEPS, 2, SPECIES, BY, BZ), F32),
            pltpu.VMEM((STEPS, 2, SPECIES, BX, BZ), F32),
            pltpu.VMEM((STEPS, 2, SPECIES, BX, BZ), F32),
            pltpu.VMEM((STEPS, 2, SPECIES // 2, 8, BZ), F32),
            pltpu.VMEM((STEPS, 2, SPECIES // 2, 8, BZ), F32),
            pltpu.VMEM((SPECIES, 8, BZ), F32),
            pltpu.VMEM((SPECIES, 8, BZ), F32),
            pltpu.VMEM((SPECIES, 8, BZ), F32),
            pltpu.SemaphoreType.DMA((5,)),
            pltpu.SemaphoreType.DMA((BX,)),
            pltpu.SemaphoreType.DMA((2,)),
            pltpu.SemaphoreType.DMA((2,)),
            pltpu.SemaphoreType.DMA,
            pltpu.SemaphoreType.DMA((2,)),
            pltpu.SemaphoreType.DMA((2,)),
            pltpu.SemaphoreType.DMA((2,)),
            pltpu.SemaphoreType.DMA((STEPS + 1, 6)),
            pltpu.SemaphoreType.DMA((STEPS + 1, 6)),
        ],
        compiler_params=pltpu.CompilerParams(
            collective_id=0, has_side_effects=True, vmem_limit_bytes=60 * 1024 * 1024
        ),
    )(
        terminal_adjoint.reshape(SPECIES, BX, BY, BZ),
        diffusivity.reshape(brick),
        velocity.reshape(flow),
        charge_modes.reshape(BX, PY, MODES),
        jnp.asarray(high),
        jnp.asarray(low),
    )
    return out.reshape(terminal_adjoint.shape)


def solution(mesh):
    return jax.shard_map(
        body,
        mesh=mesh,
        in_specs=(
            P(None, "gx", None, "yz", None),
            P(None, "gx", None, "yz", None),
            P(None, "gx", None, "yz", None),
            P("gx", "yz", None, None),
        ),
        out_specs=P(None, "gx", None, "yz", None),
        check_vma=False,
    )
```

```python
import functools
import math

import jax
import jax.numpy as jnp
import ml_dtypes
import numpy as np
from jax import lax
from jax.experimental import pallas as pl
from jax.experimental.pallas import tpu as pltpu
from jax.sharding import PartitionSpec as P

SPECIES = 4
STEPS = 3
SCREEN = 1.0
MESH = pl.DeviceIdType.MESH

PZ, PY = 4, 16
NYZ = PZ * PY
BX, BY, BZ = 8, 64, 128
MODES = 512
TOP, ROWS = 8, 80
TILE = BX + 1
PLACE = {x: (x + 1) % BX for x in range(BX)}
FACE = 2
LOW, HIGH = NYZ, NYZ + 1
HALF = 32
F32, BF16 = jnp.float32, jnp.bfloat16


def base_table():
    half = MODES // 2
    modes = np.arange(half)[:, None]
    cells = np.arange(BZ)[None, :]
    angle = (modes * cells % MODES) * (2.0 * math.pi / MODES)
    theta = modes * (2.0 * math.pi / MODES)
    green = 1.0 / (1.0 + SCREEN * theta * theta)
    table = np.concatenate([np.cos(angle) * green, np.sin(angle) * green], 0)
    high = table.astype(np.float32).astype(ml_dtypes.bfloat16)
    low = (table - high.astype(np.float64)).astype(ml_dtypes.bfloat16)
    return high, low


def quarter_turned(a, b, turns):
    if turns == 0:
        return a, b
    k = lax.broadcasted_iota(jnp.int32, a.shape, 1)
    odd = (k & 1) == 1
    if turns == 2:
        return jnp.where(odd, -a, a), jnp.where(odd, -b, b)
    third = (k & 2) == 2
    if turns == 3:
        third = third != odd
    cos_part = jnp.where(odd, b, a)
    sin_part = jnp.where(odd, a, b)
    cos_part = jnp.where(third, -cos_part, cos_part)
    sin_part = jnp.where(third != odd, -sin_part, sin_part)
    return cos_part, sin_part


def lanes():
    return lax.broadcasted_iota(jnp.int32, (8, BZ), 1)


def pack(packed, tile_of, places):
    slot = ((lanes() + 1) >> 1) & (BX * 8 - 1)
    for x, r in places:
        i = 8 * x + r
        tile = tile_of(x, r)
        packed = jnp.where(slot == i, pltpu.roll(tile, 2 * i, 1) if i else tile, packed)
    return packed


def unpack(packed, x, r):
    lane = lanes()
    i = 8 * x + r
    moved = pltpu.roll(packed, BZ - 2 * i, 1) if i else packed
    return jnp.where((lane == 0) | (lane == BZ - 1), moved, 0.0)


EVERY = tuple((x, r) for x in range(BX) for r in range(8))
INNER = tuple((x, r) for x, r in EVERY if 0 < x < BX - 1 and 0 < r < 7)
OUTER = tuple(place for place in EVERY if place not in INNER)
FACES = tuple(place for place in EVERY if place[0] in (0, BX - 1))
EDGES = tuple(place for place in OUTER if place not in FACES)


def padded_row(x):
    return (x + 1) * ROWS + TOP


def slab_kernel(
    lam_hbm, dif_hbm, vel_hbm, cm_hbm, high_hbm, low_hbm, l3,
    l0, l1, l2, dif, vel, along, base, grad, slope, pot, cm, high, low,
    product, sendbuf, recv, x_in, y_out, y_in, z_out, z_in, pot_in, packs, factors, came,
    load_sem, lam_sem, a2a_send, a2a_recv, edge_send, edge_recv, pass_send, pass_recv, halo_send, halo_recv,
):
    gx = lax.axis_index("gx")
    me = lax.axis_index("yz")
    ngx = lax.axis_size("gx")
    p = me & (PY - 1)
    zb = me >> 4
    mx, mz, my = me & 3, (me >> 2) & 7, me >> 5
    has = {
        "x+": gx < ngx - 1, "x-": gx > 0,
        "y+": p < PY - 1, "y-": p > 0,
        "z+": zb < PZ - 1, "z-": zb > 0,
    }
    ids = {
        "x+": {"gx": gx + 1}, "x-": {"gx": gx - 1},
        "y+": {"yz": me + 1}, "y-": {"yz": me - 1},
        "z+": {"yz": me + PY}, "z-": {"yz": me - PY},
    }
    ways = ("z+", "z-", "x+", "x-", "y+", "y-")
    back = {"x+": "x-", "x-": "x+", "y+": "y-", "y-": "y+", "z+": "z-", "z-": "z+"}

    def partners(act):
        @pl.loop(0, 8)
        def _(j):
            step = (j + 1) >> 1
            z = (mz + 4 + jnp.where((j & 1) == 0, -step, step)) & 7
            for dx in (2, 1, 3, 0):
                for dy in (1, 0):
                    x = (mx + dx) & 3
                    y = 1 - my if dy else my
                    peer = (y * 8 + z) * 4 + x
                    if dx or dy:
                        act(peer)
                    else:
                        pl.when(j < 7)(functools.partial(act, peer))

    barrier = pltpu.get_barrier_semaphore()
    partners(
        lambda peer: pl.semaphore_signal(
            barrier, inc=1, device_id={"yz": peer}, device_id_type=MESH
        )
    )
    for way in ("x+", "x-"):
        @pl.when(has[way])
        def _():
            pl.semaphore_signal(barrier, inc=1, device_id=ids[way], device_id_type=MESH)

    loads = [
        pltpu.make_async_copy(cm_hbm, cm, load_sem.at[0]),
        pltpu.make_async_copy(high_hbm, high, load_sem.at[1]),
        pltpu.make_async_copy(low_hbm, low, load_sem.at[2]),
        pltpu.make_async_copy(dif_hbm, dif, load_sem.at[3]),
        pltpu.make_async_copy(vel_hbm, vel, load_sem.at[4]),
    ]
    lam_loads = [
        pltpu.make_async_copy(lam_hbm.at[:, x], l0.at[:, pl.ds(padded_row(x), BY), :], lam_sem.at[x])
        for x in range(BX)
    ]
    for load in loads[:3] + lam_loads + loads[3:]:
        load.start()

    zero = jnp.zeros((BY, BZ), F32)
    line = jnp.zeros((BX, BZ), F32)
    for ref in (l0, l1, l2):
        @pl.loop(0, SPECIES)
        def _(s):
            ref[s, TOP : TOP + BY, :] = zero
            ref[s, padded_row(BX) : padded_row(BX) + BY, :] = zero
            ref[s, pl.ds(padded_row(0) - 1, BX, stride=ROWS), :] = line
            ref[s, pl.ds(padded_row(0) + BY, BX, stride=ROWS), :] = line

    pot[0, TOP : TOP + BY, :] = zero
    pot[0, padded_row(BX) : padded_row(BX) + BY, :] = zero
    pot[0, pl.ds(padded_row(0) - 1, BX, stride=ROWS), :] = line
    pot[0, pl.ds(padded_row(0) + BY, BX, stride=ROWS), :] = line

    for side, way in enumerate(("-", "+")):
        @pl.when(jnp.logical_not(has["x" + way]))
        def _():
            for stage in range(STEPS):
                for s in range(SPECIES):
                    x_in[stage, side, s] = zero
            pot_in[side, 0] = zero

        @pl.when(jnp.logical_not(has["y" + way]))
        def _():
            for stage in range(STEPS):
                for s in range(SPECIES):
                    y_in[stage, side, s] = line
            recv[(LOW + side) * TILE : (LOW + side) * TILE + BX, :] = line

        @pl.when(jnp.logical_not(has["z" + way]))
        def _():
            for stage in range(STEPS):
                for pair in range(SPECIES // 2):
                    z_in[stage, side, pair] = line

    for load in loads[:3]:
        load.wait()
    charge = cm[...].reshape(BX * PY, MODES)
    a, b = charge[:, : MODES // 2], charge[:, MODES // 2 :]
    dot = functools.partial(jnp.dot, preferred_element_type=F32)
    rims_of = []
    for turns in range(PZ):
        total = None
        for half, part in enumerate(quarter_turned(a, b, turns)):
            rows = slice(half * MODES // 2, (half + 1) * MODES // 2)
            part_high = part.astype(BF16)
            part_low = (part - part_high.astype(F32)).astype(BF16)
            term = dot(part_high, high[rows, :]) + (
                dot(part_low, high[rows, :]) + dot(part_high, low[rows, :])
            )
            total = term if total is None else total + term
        product[turns] = total
        turned = jnp.transpose(total)
        rims_of.append((turned[:1], turned[BZ - 1 :]))
        for q in range(PY):
            at = (turns * PY + q) * TILE
            sendbuf[pl.ds(at, BX), :] = pltpu.roll(product[turns, pl.ds(q, BX, stride=PY), :], 1, 0)
    nothing = jnp.zeros((1, BZ), F32)
    odd = (lax.broadcasted_iota(jnp.int32, (1, BZ), 1) & 1) == 1
    for layer in range(PZ):
        below = rims_of[layer - 1][1] if layer > 0 else nothing
        above = rims_of[layer + 1][0] if layer < PZ - 1 else nothing
        above = pltpu.roll(above, BZ - 1, 1)
        rows = (jnp.where(odd, above, below), jnp.where(odd, below, above))
        for q in range(PY):
            at = (layer * PY + q) * TILE + BX
            sendbuf[at : at + 1, :] = rows[q % 2]

    def halo_copy(stage, way, fields):
        number = ways.index(way)
        side = 0 if way[1] == "+" else 1
        if way[0] == "x":
            src = fields.at[:, pl.ds(padded_row(BX - 1 if side == 0 else 0), BY), :]
            if stage == STEPS:
                dst = pot_in.at[side]
            else:
                dst = x_in.at[stage, side]
        elif way[0] == "y":
            src, dst = y_out.at[stage, side], y_in.at[stage, side]
        else:
            src, dst = z_out.at[stage, side], z_in.at[stage, side]
        return pltpu.make_async_remote_copy(
            src_ref=src, dst_ref=dst,
            send_sem=halo_send.at[stage, number], recv_sem=halo_recv.at[stage, number],
            device_id=ids[way], device_id_type=MESH,
        )

    def start(stage, fields, which=ways):
        for way in which:
            pl.when(has[way])(lambda: halo_copy(stage, way, fields).start())

    def receive(stage, fields, which=ways):
        for way in which:
            pl.when(has[back[way]])(lambda: halo_copy(stage, way, fields).wait_recv())

    def finish(stage, fields, which=ways):
        for way in which:
            pl.when(has[way])(lambda: halo_copy(stage, way, fields).wait_send())

    def own_tiles(fields, s):
        def tile_of(x, r):
            row = padded_row(x) + 8 * r
            return fields[s, row : row + 8, :]
        return tile_of

    even = (lanes() & 1) == 0

    def send_lanes(stage, fields, packed):
        for pair in range(SPECIES // 2):
            one, two = packed(2 * pair), packed(2 * pair + 1)
            z_out[stage, 0, pair] = jnp.where(even, pltpu.roll(two, 1, 1), one)
            z_out[stage, 1, pair] = jnp.where(even, one, pltpu.roll(two, BZ - 1, 1))
        start(stage, fields, ("z+", "z-"))

    def receive_lanes(stage, fields):
        receive(stage, fields, ("z+", "z-"))
        for pair in range(SPECIES // 2):
            below, above = z_in[stage, 0, pair], z_in[stage, 1, pair]
            came[2 * pair] = jnp.where(even, pltpu.roll(below, 1, 1), pltpu.roll(above, BZ - 1, 1))
            came[2 * pair + 1] = jnp.where(even, below, above)

    def send_rows(stage, fields):
        for s in range(SPECIES):
            y_out[stage, 0, s] = fields[s, pl.ds(padded_row(0) + BY - 1, BX, stride=ROWS), :]
            y_out[stage, 1, s] = fields[s, pl.ds(padded_row(0), BX, stride=ROWS), :]
        start(stage, fields, ("y+", "y-"))

    lane = lax.broadcasted_iota(jnp.int32, (BY, BZ), 1)
    tile_low = lanes() == 0
    half_low, half_high = lane[:HALF] == 0, lane[:HALF] == BZ - 1

    def differences(fields, s, x, y):
        r = padded_row(x) + y
        centre = fields[s, r : r + HALF, :]
        x_plus, x_minus = fields[s, r + ROWS : r + ROWS + HALF, :], fields[s, r - ROWS : r - ROWS + HALF, :]
        y_plus, y_minus = fields[s, r + 1 : r + 1 + HALF, :], fields[s, r - 1 : r - 1 + HALF, :]
        z_plus = jnp.where(half_high, 0.0, pltpu.roll(centre, BZ - 1, 1))
        z_minus = jnp.where(half_low, 0.0, pltpu.roll(centre, 1, 1))
        spread = (x_plus + x_minus) + (y_plus + y_minus) + (z_plus + z_minus) - 6.0 * centre
        return centre, spread, (x_plus - x_minus, y_plus - y_minus, z_plus - z_minus)

    def quarter_valence(s):
        return jnp.where(s == 0, 0.25, jnp.where(s == 2, 0.5, -0.25)).astype(F32)

    def pack_first():
        for load in lam_loads:
            load.wait()

        @pl.loop(0, SPECIES // 2)
        def _(pair):
            for s in (2 * pair, 2 * pair + 1):
                packs[s] = pack(line, own_tiles(l0, s), EVERY)

    def first_own(begin, end):
        @pl.loop(begin, end)
        def _(s):
            charge_of = quarter_valence(s)
            for x in range(BX):
                for y in range(0, BY, HALF):
                    rows = slice(x * BY + y, x * BY + y + HALF)
                    centre, spread, diff = differences(l0, s, x, y)
                    diffusion = dif[s, rows, :]
                    scaled = charge_of * diffusion
                    total = centre + diffusion * spread
                    for axis in range(3):
                        total = total + (0.5 * vel[axis, rows, :]) * diff[axis]
                        grad[axis, s, rows, :] = scaled * diff[axis]
                    base[s, rows, :] = total

    def load_rest():
        for load in loads[3:]:
            load.wait()

    ahead = mz < 4
    behind = jnp.logical_not(ahead)

    @pl.when(ahead)
    def _():
        pack_first()
        load_rest()
        first_own(0, SPECIES)

    pl.semaphore_wait(
        barrier,
        NYZ - 1 + has["x+"].astype(jnp.int32) + has["x-"].astype(jnp.int32),
    )

    def part(ref, index, start, count):
        return ref.at[pl.ds(index * TILE + start, count), :]

    def send_part(number, start, count):
        def act(peer):
            pltpu.make_async_remote_copy(
                src_ref=part(sendbuf, peer, start, count),
                dst_ref=part(recv, me, start, count),
                send_sem=a2a_send.at[number], recv_sem=a2a_recv.at[number],
                device_id={"yz": peer}, device_id_type=MESH,
            ).start()
        return act

    def bytes_of(ref, rows, sem):
        return pltpu.make_async_copy(ref.at[pl.ds(0, rows), :], ref.at[pl.ds(0, rows), :], sem)

    first, last = me == 0, me == NYZ - 1
    special = first | last

    def edge_tile(peer, side):
        return pltpu.make_async_remote_copy(
            src_ref=part(sendbuf, peer, FACE, TILE - FACE), dst_ref=part(recv, me, FACE, TILE - FACE),
            send_sem=edge_send, recv_sem=edge_recv.at[side],
            device_id={"yz": peer}, device_id_type=MESH,
        )

    def pass_on(side):
        return pltpu.make_async_remote_copy(
            src_ref=part(recv, (NYZ - 1) * (1 - side), 0, BX), dst_ref=part(recv, LOW + side, 0, BX),
            send_sem=pass_send.at[side], recv_sem=pass_recv.at[side],
            device_id=ids["y-" if side else "y+"], device_id_type=MESH,
        )

    mine = pl.ds(me * TILE, TILE)
    recv[mine, :] = sendbuf[mine, :]
    partners(send_part(0, 0, FACE))
    pl.when(last)(lambda: partners(lambda peer: edge_tile(peer, 0).start()))
    pl.when(first)(lambda: partners(lambda peer: edge_tile(peer, 1).start()))

    pl.when(behind)(pack_first)
    send_lanes(0, l0, lambda s: packs[s])
    start(0, l0, ("x+", "x-"))
    send_rows(0, l0)
    pl.when(jnp.logical_not(special) & ahead)(lambda: partners(send_part(1, FACE, TILE - FACE)))

    @pl.when(behind)
    def _():
        load_rest()
        first_own(0, SPECIES)

    pl.when(jnp.logical_not(special) & behind)(lambda: partners(send_part(1, FACE, TILE - FACE)))

    bytes_of(recv, (NYZ - 1) * FACE, a2a_recv.at[0]).wait()

    def assemble(x):
        pot[0, padded_row(x) : padded_row(x) + BY, :] = recv[pl.ds(PLACE[x], BY, stride=TILE), :]

    assemble(0)
    assemble(BX - 1)
    start(STEPS, pot, ("x+", "x-"))
    pl.when(jnp.logical_not(last))(lambda: edge_tile(lax.rem(me + 1, NYZ), 0).wait_recv())
    pl.when(jnp.logical_not(first))(lambda: edge_tile(lax.rem(me + 1, NYZ), 1).wait_recv())
    pl.when(has["y+"])(lambda: pass_on(0).start())
    pl.when(has["y-"])(lambda: pass_on(1).start())

    def rim_terms(axis, side, s, rows):
        diffusion, flow = dif[s, rows, :], 0.5 * vel[axis, rows, :]
        scaled = quarter_valence(s) * diffusion
        if side == 0:
            return diffusion - flow, -scaled
        return diffusion + flow, scaled

    receive(0, l0, ("x+", "x-", "y+", "y-"))
    receive_lanes(0, l0)

    @pl.loop(0, SPECIES)
    def _(s):
        for side in (0, 1):
            x = (BX - 1) * side
            rows = slice(x * BY, (x + 1) * BY)
            value = x_in[0, side, s]
            to_base, to_grad = rim_terms(0, side, s, rows)
            base[s, rows, :] += to_base * value
            grad[0, s, rows, :] += to_grad * value
            rows = pl.ds((BY - 1) * side, BX, stride=BY)
            value = y_in[0, side, s]
            to_base, to_grad = rim_terms(1, side, s, rows)
            base[s, rows, :] += to_base * value
            grad[1, s, rows, :] += to_grad * value
        for x, r in EVERY:
            rows = slice(x * BY + 8 * r, x * BY + 8 * r + 8)
            value = unpack(came[s], x, r)
            diffusion, flow = dif[s, rows, :], 0.5 * vel[2, rows, :]
            scaled = quarter_valence(s) * diffusion
            base[s, rows, :] += (diffusion + jnp.where(tile_low, -flow, flow)) * value
            grad[2, s, rows, :] += jnp.where(tile_low, -scaled, scaled) * value

    pl.when(special)(
        lambda: bytes_of(recv, (NYZ - 2) * (TILE - FACE), a2a_recv.at[1]).wait()
    )
    pl.when(jnp.logical_not(special))(
        lambda: bytes_of(recv, (NYZ - 3) * (TILE - FACE), a2a_recv.at[1]).wait()
    )
    for x in range(1, BX - 1):
        assemble(x)
    z_rims = pltpu.roll(recv[pl.ds(BX, BY, stride=TILE), :], (BZ - p) & (BZ - 1), 1)

    def first_step(x):
        rims_here = pltpu.roll(z_rims, BZ - 16 * x, 1) if x else z_rims
        for y in range(0, BY, HALF):
            r = padded_row(x) + y
            rows = slice(x * BY + y, x * BY + y + HALF)
            centre = pot[0, r : r + HALF, :]
            rim = rims_here[y : y + HALF]
            z_plus = jnp.where(half_high, rim, pltpu.roll(centre, BZ - 1, 1))
            z_minus = jnp.where(half_low, rim, pltpu.roll(centre, 1, 1))
            here = (
                pot[0, r + ROWS : r + ROWS + HALF, :] - pot[0, r - ROWS : r - ROWS + HALF, :],
                pot[0, r + 1 : r + 1 + HALF, :] - pot[0, r - 1 : r - 1 + HALF, :],
                z_plus - z_minus,
            )
            for axis in range(3):
                slope[axis, rows, :] = here[axis]
            for s in range(SPECIES):
                total = base[s, rows, :]
                for axis in range(3):
                    total = total - here[axis] * grad[axis, s, rows, :]
                l1[s, r : r + HALF, :] = total

    for x in range(BX):
        first_step(x)
    packed = [pack(line, own_tiles(l1, s), INNER) for s in range(SPECIES)]
    pl.when(has["y-"])(lambda: pass_on(0).wait_recv())
    pl.when(has["y+"])(lambda: pass_on(1).wait_recv())
    for side in (0, 1):
        at = (LOW + side) * TILE
        change = pltpu.roll(recv[at : at + BX, :], BX - 1, 0)
        change = change if side else -change
        rows = pl.ds((BY - 1) * side, BX, stride=BY)
        padded_rows = pl.ds(padded_row(0) + (BY - 1) * side, BX, stride=ROWS)
        slope[1, rows, :] += change
        for s in range(SPECIES):
            l1[s, padded_rows, :] -= change * grad[1, s, rows, :]
    packed = [pack(packed[s], own_tiles(l1, s), EDGES) for s in range(SPECIES)]
    receive(STEPS, pot, ("x+", "x-"))
    for side in (0, 1):
        x = (BX - 1) * side
        change = -pot_in[side, 0] if side else pot_in[side, 0]
        rows = slice(x * BY, (x + 1) * BY)
        for s in range(SPECIES):
            l1[s, padded_row(x) : padded_row(x) + BY, :] += change * grad[0, s, rows, :]
    start(1, l1, ("x+", "x-"))
    packed = [pack(packed[s], own_tiles(l1, s), FACES) for s in range(SPECIES)]
    send_lanes(1, l1, lambda s: packed[s])
    send_rows(1, l1)
    for side in (0, 1):
        rows = slice((BX - 1) * side * BY, ((BX - 1) * side + 1) * BY)
        slope[0, rows, :] += pot_in[side, 0] if side else -pot_in[side, 0]

    def own_values(step, now, later, row_of):
        @pl.loop(0, SPECIES)
        def _(s):
            charge_of = quarter_valence(s)
            for x in range(BX):
                for y in range(0, BY, HALF):
                    rows = slice(x * BY + y, x * BY + y + HALF)
                    centre, spread, diff = differences(now, s, x, y)
                    diffusion = dif[s, rows, :]
                    total = centre + diffusion * spread
                    scaled = charge_of * diffusion
                    for axis in range(3):
                        if step == 1:
                            rate = 0.5 * vel[axis, rows, :] - scaled * slope[axis, rows, :]
                            along[axis, s, rows, :] = rate
                        else:
                            rate = along[axis, s, rows, :]
                        total = total + rate * diff[axis]
                    r = row_of(x) + y
                    later[s, r : r + HALF, :] = total

    def x_values(step, later, row_of):
        for s in range(SPECIES):
            for side in (0, 1):
                x = (BX - 1) * side
                rows = slice(x * BY, (x + 1) * BY)
                rate = along[0, s, rows, :]
                factor = dif[s, rows, :] + (rate if side else -rate)
                later[s, row_of(x) : row_of(x) + BY, :] += factor * x_in[step, side, s]

    def y_values(step, later, row_of):
        apart = row_of(1) - row_of(0)
        for s in range(SPECIES):
            for side in (0, 1):
                rows = pl.ds((BY - 1) * side, BX, stride=BY)
                rate = along[1, s, rows, :]
                factor = dif[s, rows, :] + (rate if side else -rate)
                later[s, pl.ds(row_of(0) + (BY - 1) * side, BX, stride=apart), :] += factor * y_in[step, side, s]

    def lane_factor(s):
        def tile_of(x, r):
            rows = slice(x * BY + 8 * r, x * BY + 8 * r + 8)
            rate = along[2, s, rows, :]
            return dif[s, rows, :] + jnp.where(tile_low, -rate, rate)
        return tile_of

    def lane_values(s, places, later, row_of):
        factor = lane_factor(s)
        for x, r in places:
            row = row_of(x) + 8 * r
            later[s, row : row + 8, :] += factor(x, r) * unpack(came[s], x, r)

    def by_pairs(act):
        @pl.loop(0, SPECIES // 2)
        def _(pair):
            act(2 * pair)
            act(2 * pair + 1)

    own_values(1, l1, l2, padded_row)

    def pack_factors(s):
        factors[s] = pack(line, lane_factor(s), EVERY)

    by_pairs(pack_factors)
    packed = [pack(line, own_tiles(l2, s), INNER) for s in range(SPECIES)]
    receive(1, l1, ("y+", "y-"))
    y_values(1, l2, padded_row)
    packed = [pack(packed[s], own_tiles(l2, s), EDGES) for s in range(SPECIES)]
    receive(1, l1, ("x+", "x-"))
    x_values(1, l2, padded_row)
    packed = [pack(packed[s], own_tiles(l2, s), FACES) for s in range(SPECIES)]
    receive_lanes(1, l1)
    send_lanes(2, l2, lambda s: packed[s] + factors[s] * came[s])
    for s in range(SPECIES):
        lane_values(s, FACES, l2, padded_row)
    start(2, l2, ("x+", "x-"))
    for s in range(SPECIES):
        lane_values(s, EDGES, l2, padded_row)
    send_rows(2, l2)
    by_pairs(lambda s: lane_values(s, INNER, l2, padded_row))

    flat_row = lambda x: x * BY
    own_values(2, l2, l3, flat_row)
    receive(2, l2, ("y+", "y-"))
    y_values(2, l3, flat_row)
    receive_lanes(2, l2)

    by_pairs(lambda s: lane_values(s, EVERY, l3, flat_row))
    receive(2, l2, ("x+", "x-"))
    x_values(2, l3, flat_row)

    @pl.when(special)
    def _():
        bytes_of(sendbuf, (NYZ - 1) * (TILE - FACE), edge_send).wait()

    bytes_of(sendbuf, (NYZ - 1) * FACE, a2a_send.at[0]).wait()

    @pl.when(jnp.logical_not(special))
    def _():
        bytes_of(sendbuf, (NYZ - 1) * (TILE - FACE), a2a_send.at[1]).wait()

    pl.when(has["y+"])(lambda: pass_on(0).wait_send())
    pl.when(has["y-"])(lambda: pass_on(1).wait_send())
    for stage, ref in enumerate((l0, l1, l2)):
        finish(stage, ref)
    finish(STEPS, pot, ("x+", "x-"))


def hand_over_kernel(source, target, sems):
    copies = [
        pltpu.make_async_copy(source.at[s], target.at[s], sems.at[s]) for s in range(SPECIES)
    ]
    for copy in copies:
        copy.start()
    for copy in copies:
        copy.wait()


def body(terminal_adjoint, diffusivity, velocity, charge_modes):
    high, low = base_table()
    cells = BX * BY
    brick = (SPECIES, cells, BZ)
    padded = (SPECIES, (BX + 2) * ROWS, BZ)
    flow = (3, cells, BZ)
    anywhere = pl.BlockSpec(memory_space=pl.ANY)
    out = pl.pallas_call(
        slab_kernel,
        out_shape=pltpu.VMEM(brick, F32),
        in_specs=[anywhere] * 6,
        out_specs=pl.BlockSpec(memory_space=pltpu.VMEM),
        scratch_shapes=[
            pltpu.VMEM(padded, F32), pltpu.VMEM(padded, F32), pltpu.VMEM(padded, F32),
            pltpu.VMEM(brick, F32),
            pltpu.VMEM(flow, F32),
            pltpu.VMEM((3,) + brick, F32),
            pltpu.VMEM(brick, F32),
            pltpu.VMEM((3,) + brick, F32),
            pltpu.VMEM(flow, F32),
            pltpu.VMEM((1,) + padded[1:], F32),
            pltpu.VMEM((BX, PY, MODES), F32),
            pltpu.VMEM((MODES, BZ), BF16), pltpu.VMEM((MODES, BZ), BF16),
            pltpu.VMEM((PZ, BX * PY, BZ), F32),
            pltpu.VMEM((NYZ * TILE, BZ), F32),
            pltpu.VMEM(((NYZ + 2) * TILE, BZ), F32),
            pltpu.VMEM((STEPS, 2, SPECIES, BY, BZ), F32),
            pltpu.VMEM((STEPS, 2, SPECIES, BX, BZ), F32),
            pltpu.VMEM((STEPS, 2, SPECIES, BX, BZ), F32),
            pltpu.VMEM((STEPS, 2, SPECIES // 2, 8, BZ), F32),
            pltpu.VMEM((STEPS, 2, SPECIES // 2, 8, BZ), F32),
            pltpu.VMEM((2, 1, BY, BZ), F32),
            pltpu.VMEM((SPECIES, 8, BZ), F32),
            pltpu.VMEM((SPECIES, 8, BZ), F32),
            pltpu.VMEM((SPECIES, 8, BZ), F32),
            pltpu.SemaphoreType.DMA((5,)),
            pltpu.SemaphoreType.DMA((BX,)),
            pltpu.SemaphoreType.DMA((2,)),
            pltpu.SemaphoreType.DMA((2,)),
            pltpu.SemaphoreType.DMA,
            pltpu.SemaphoreType.DMA((2,)),
            pltpu.SemaphoreType.DMA((2,)),
            pltpu.SemaphoreType.DMA((2,)),
            pltpu.SemaphoreType.DMA((STEPS + 1, 6)),
            pltpu.SemaphoreType.DMA((STEPS + 1, 6)),
        ],
        compiler_params=pltpu.CompilerParams(
            collective_id=0, has_side_effects=True, vmem_limit_bytes=60 * 1024 * 1024
        ),
    )(
        terminal_adjoint.reshape(SPECIES, BX, BY, BZ),
        diffusivity.reshape(brick),
        velocity.reshape(flow),
        charge_modes.reshape(BX, PY, MODES),
        jnp.asarray(high),
        jnp.asarray(low),
    )
    return out.reshape(terminal_adjoint.shape)


def solution(mesh):
    return jax.shard_map(
        body,
        mesh=mesh,
        in_specs=(
            P(None, "gx", None, "yz", None),
            P(None, "gx", None, "yz", None),
            P(None, "gx", None, "yz", None),
            P("gx", "yz", None, None),
        ),
        out_specs=P(None, "gx", None, "yz", None),
        check_vma=False,
    )
```

```python
import functools
import math

import jax
import jax.numpy as jnp
import ml_dtypes
import numpy as np
from jax import lax
from jax.experimental import pallas as pl
from jax.experimental.pallas import tpu as pltpu
from jax.sharding import PartitionSpec as P

SPECIES = 4
STEPS = 3
SCREEN = 1.0
MESH = pl.DeviceIdType.MESH

PZ, PY = 4, 16
NYZ = PZ * PY
BX, BY, BZ = 8, 64, 128
MODES = 512
TOP, ROWS = 8, 80
TILE = BX + 1
PLACE = {x: (x + 1) % BX for x in range(BX)}
FACE = 2
LOW, HIGH = NYZ, NYZ + 1
HALF = 32
F32, BF16 = jnp.float32, jnp.bfloat16


def base_table():
    half = MODES // 2
    modes = np.arange(half)[:, None]
    cells = np.arange(BZ)[None, :]
    angle = (modes * cells % MODES) * (2.0 * math.pi / MODES)
    theta = modes * (2.0 * math.pi / MODES)
    green = 1.0 / (1.0 + SCREEN * theta * theta)
    table = np.concatenate([np.cos(angle) * green, np.sin(angle) * green], 0)
    high = table.astype(np.float32).astype(ml_dtypes.bfloat16)
    low = (table - high.astype(np.float64)).astype(ml_dtypes.bfloat16)
    return high, low


def quarter_turned(a, b, turns):
    if turns == 0:
        return a, b
    k = lax.broadcasted_iota(jnp.int32, a.shape, 1)
    odd = (k & 1) == 1
    if turns == 2:
        return jnp.where(odd, -a, a), jnp.where(odd, -b, b)
    third = (k & 2) == 2
    if turns == 3:
        third = third != odd
    cos_part = jnp.where(odd, b, a)
    sin_part = jnp.where(odd, a, b)
    cos_part = jnp.where(third, -cos_part, cos_part)
    sin_part = jnp.where(third != odd, -sin_part, sin_part)
    return cos_part, sin_part


def lanes():
    return lax.broadcasted_iota(jnp.int32, (8, BZ), 1)


def pack(packed, tile_of, places):
    slot = ((lanes() + 1) >> 1) & (BX * 8 - 1)
    for x, r in places:
        i = 8 * x + r
        tile = tile_of(x, r)
        packed = jnp.where(slot == i, pltpu.roll(tile, 2 * i, 1) if i else tile, packed)
    return packed


def unpack(packed, x, r):
    lane = lanes()
    i = 8 * x + r
    moved = pltpu.roll(packed, BZ - 2 * i, 1) if i else packed
    return jnp.where((lane == 0) | (lane == BZ - 1), moved, 0.0)


EVERY = tuple((x, r) for x in range(BX) for r in range(8))
INNER = tuple((x, r) for x, r in EVERY if 0 < x < BX - 1 and 0 < r < 7)
OUTER = tuple(place for place in EVERY if place not in INNER)
FACES = tuple(place for place in EVERY if place[0] in (0, BX - 1))
EDGES = tuple(place for place in OUTER if place not in FACES)


def padded_row(x):
    return (x + 1) * ROWS + TOP


def slab_kernel(
    lam_hbm, dif_hbm, vel_hbm, cm_hbm, high_hbm, low_hbm, l3,
    l0, l1, l2, dif, vel, along, base, grad, slope, pot, cm, high, low,
    product, sendbuf, recv, x_in, y_out, y_in, z_out, z_in, pot_in, side_out, side_in, packs, factors, x_factors, came,
    load_sem, lam_sem, a2a_send, a2a_recv, edge_send, edge_recv, pass_send, pass_recv, group_in, far_send, far_recv, halo_send, halo_recv,
):
    gx = lax.axis_index("gx")
    me = lax.axis_index("yz")
    ngx = lax.axis_size("gx")
    p = me & (PY - 1)
    zb = me >> 4
    mx, mz, my = me & 3, (me >> 2) & 7, me >> 5
    has = {
        "x+": gx < ngx - 1, "x-": gx > 0,
        "y+": p < PY - 1, "y-": p > 0,
        "z+": zb < PZ - 1, "z-": zb > 0,
    }
    ids = {
        "x+": {"gx": gx + 1}, "x-": {"gx": gx - 1},
        "y+": {"yz": me + 1}, "y-": {"yz": me - 1},
        "z+": {"yz": me + PY}, "z-": {"yz": me - PY},
    }
    lower, upper = gx == 1, gx == 2
    far_gx = jnp.where(lower, 2, 1)
    middle = lower | upper
    for way in "+-":
        has["l" + way], ids["l" + way] = has["x" + way], ids["x" + way]
    ways = ("z+", "z-", "x+", "x-", "y+", "y-")
    numbers = ways + ("l+", "l-")
    back = {"x+": "x-", "x-": "x+", "y+": "y-", "y-": "y+", "z+": "z-", "z-": "z+", "l+": "l-", "l-": "l+"}

    def partners(act):
        @pl.loop(0, 8)
        def _(j):
            step = (j + 1) >> 1
            z = (mz + 4 + jnp.where((j & 1) == 0, -step, step)) & 7
            for dx in (2, 1, 3, 0):
                for dy in (1, 0):
                    x = (mx + dx) & 3
                    y = 1 - my if dy else my
                    peer = (y * 8 + z) * 4 + x
                    if dx or dy:
                        act(peer)
                    else:
                        pl.when(j < 7)(functools.partial(act, peer))

    loads = [
        pltpu.make_async_copy(cm_hbm, cm, load_sem.at[0]),
        pltpu.make_async_copy(high_hbm, high, load_sem.at[1]),
        pltpu.make_async_copy(low_hbm, low, load_sem.at[2]),
        pltpu.make_async_copy(dif_hbm, dif, load_sem.at[3]),
        pltpu.make_async_copy(vel_hbm, vel, load_sem.at[4]),
    ]
    lam_loads = [
        pltpu.make_async_copy(lam_hbm.at[:, x], l0.at[:, pl.ds(padded_row(x), BY), :], lam_sem.at[x])
        for x in range(BX)
    ]
    for load in loads[:3]:
        load.start()

    barrier = pltpu.get_barrier_semaphore()
    partners(
        lambda peer: pl.semaphore_signal(
            barrier, inc=1, device_id={"yz": peer}, device_id_type=MESH
        )
    )
    for way in ("x+", "x-"):
        @pl.when(has[way])
        def _():
            pl.semaphore_signal(barrier, inc=1, device_id=ids[way], device_id_type=MESH)

    for load in lam_loads + loads[3:]:
        load.start()

    zero = jnp.zeros((BY, BZ), F32)
    line = jnp.zeros((BX, BZ), F32)
    for ref in (l0, l1, l2):
        @pl.loop(0, SPECIES)
        def _(s):
            ref[s, TOP : TOP + BY, :] = zero
            ref[s, padded_row(BX) : padded_row(BX) + BY, :] = zero
            ref[s, pl.ds(padded_row(0) - 1, BX, stride=ROWS), :] = line
            ref[s, pl.ds(padded_row(0) + BY, BX, stride=ROWS), :] = line

    pot[0, TOP : TOP + BY, :] = zero
    pot[0, padded_row(BX) : padded_row(BX) + BY, :] = zero
    pot[0, pl.ds(padded_row(0) - 1, BX, stride=ROWS), :] = line
    pot[0, pl.ds(padded_row(0) + BY, BX, stride=ROWS), :] = line

    for side, way in enumerate(("-", "+")):
        @pl.when(jnp.logical_not(has["x" + way]))
        def _():
            for stage in range(STEPS):
                for s in range(SPECIES):
                    x_in[stage, side, s] = zero
            pot_in[side, 0] = zero
            for s in range(SPECIES):
                side_in[side, s] = line

        @pl.when(jnp.logical_not(has["y" + way]))
        def _():
            for stage in range(STEPS):
                for s in range(SPECIES):
                    y_in[stage, side, s] = line
            recv[(LOW + side) * TILE : (LOW + side) * TILE + BX, :] = line

        @pl.when(jnp.logical_not(has["z" + way]))
        def _():
            for stage in range(STEPS):
                for pair in range(SPECIES // 2):
                    z_in[stage, side, pair] = line

    for load in loads[:3]:
        load.wait()
    charge = cm[...].reshape(BX * PY, MODES)
    a, b = charge[:, : MODES // 2], charge[:, MODES // 2 :]
    dot = functools.partial(jnp.dot, preferred_element_type=F32)
    rims_of = []
    for turns in range(PZ):
        total = None
        for half, part in enumerate(quarter_turned(a, b, turns)):
            rows = slice(half * MODES // 2, (half + 1) * MODES // 2)
            part_high = part.astype(BF16)
            part_low = (part - part_high.astype(F32)).astype(BF16)
            term = dot(part_high, high[rows, :]) + (
                dot(part_low, high[rows, :]) + dot(part_high, low[rows, :])
            )
            total = term if total is None else total + term
        product[turns] = total
        turned = jnp.transpose(total)
        rims_of.append((turned[:1], turned[BZ - 1 :]))
        for q in range(PY):
            at = (turns * PY + q) * TILE
            sendbuf[pl.ds(at, BX), :] = pltpu.roll(product[turns, pl.ds(q, BX, stride=PY), :], 1, 0)
    nothing = jnp.zeros((1, BZ), F32)
    odd = (lax.broadcasted_iota(jnp.int32, (1, BZ), 1) & 1) == 1
    for layer in range(PZ):
        below = rims_of[layer - 1][1] if layer > 0 else nothing
        above = rims_of[layer + 1][0] if layer < PZ - 1 else nothing
        above = pltpu.roll(above, BZ - 1, 1)
        rows = (jnp.where(odd, above, below), jnp.where(odd, below, above))
        for q in range(PY):
            at = (layer * PY + q) * TILE + BX
            sendbuf[at : at + 1, :] = rows[q % 2]

    def halo_copy(stage, way, fields):
        number = numbers.index(way)
        side = 0 if way[1] == "+" else 1
        if way[0] == "x":
            src = fields.at[:, pl.ds(padded_row(BX - 1 if side == 0 else 0), BY), :]
            if stage == STEPS:
                dst = pot_in.at[side]
            else:
                dst = x_in.at[stage, side]
        elif way[0] == "l":
            src, dst = side_out, side_in.at[side]
        elif way[0] == "y":
            src, dst = y_out.at[stage, side], y_in.at[stage, side]
        else:
            src, dst = z_out.at[stage, side], z_in.at[stage, side]
        return pltpu.make_async_remote_copy(
            src_ref=src, dst_ref=dst,
            send_sem=halo_send.at[stage, number], recv_sem=halo_recv.at[stage, number],
            device_id=ids[way], device_id_type=MESH,
        )

    def start(stage, fields, which=ways):
        for way in which:
            pl.when(has[way])(lambda: halo_copy(stage, way, fields).start())

    def receive(stage, fields, which=ways):
        for way in which:
            pl.when(has[back[way]])(lambda: halo_copy(stage, way, fields).wait_recv())

    def finish(stage, fields, which=ways):
        for way in which:
            pl.when(has[way])(lambda: halo_copy(stage, way, fields).wait_send())

    def own_tiles(fields, s):
        def tile_of(x, r):
            row = padded_row(x) + 8 * r
            return fields[s, row : row + 8, :]
        return tile_of

    even = (lanes() & 1) == 0

    def send_lanes(stage, fields, packed):
        for pair in range(SPECIES // 2):
            one, two = packed(2 * pair), packed(2 * pair + 1)
            z_out[stage, 0, pair] = jnp.where(even, pltpu.roll(two, 1, 1), one)
            z_out[stage, 1, pair] = jnp.where(even, one, pltpu.roll(two, BZ - 1, 1))
        start(stage, fields, ("z+", "z-"))

    def receive_lanes(stage, fields):
        receive(stage, fields, ("z+", "z-"))
        for pair in range(SPECIES // 2):
            below, above = z_in[stage, 0, pair], z_in[stage, 1, pair]
            came[2 * pair] = jnp.where(even, pltpu.roll(below, 1, 1), pltpu.roll(above, BZ - 1, 1))
            came[2 * pair + 1] = jnp.where(even, below, above)

    def send_rows(stage, fields):
        for s in range(SPECIES):
            y_out[stage, 0, s] = fields[s, pl.ds(padded_row(0) + BY - 1, BX, stride=ROWS), :]
            y_out[stage, 1, s] = fields[s, pl.ds(padded_row(0), BX, stride=ROWS), :]
        start(stage, fields, ("y+", "y-"))

    lane = lax.broadcasted_iota(jnp.int32, (BY, BZ), 1)
    tile_low = lanes() == 0
    half_low, half_high = lane[:HALF] == 0, lane[:HALF] == BZ - 1

    def differences(fields, s, x, y):
        r = padded_row(x) + y
        centre = fields[s, r : r + HALF, :]
        x_plus, x_minus = fields[s, r + ROWS : r + ROWS + HALF, :], fields[s, r - ROWS : r - ROWS + HALF, :]
        y_plus, y_minus = fields[s, r + 1 : r + 1 + HALF, :], fields[s, r - 1 : r - 1 + HALF, :]
        z_plus = jnp.where(half_high, 0.0, pltpu.roll(centre, BZ - 1, 1))
        z_minus = jnp.where(half_low, 0.0, pltpu.roll(centre, 1, 1))
        spread = (x_plus + x_minus) + (y_plus + y_minus) + (z_plus + z_minus) - 6.0 * centre
        return centre, spread, (x_plus - x_minus, y_plus - y_minus, z_plus - z_minus)

    def quarter_valence(s):
        return jnp.where(s == 0, 0.25, jnp.where(s == 2, 0.5, -0.25)).astype(F32)

    def pack_first():
        for load in lam_loads:
            load.wait()

        @pl.loop(0, SPECIES // 2)
        def _(pair):
            for s in (2 * pair, 2 * pair + 1):
                packs[s] = pack(line, own_tiles(l0, s), EVERY)

    def first_own(begin, end):
        @pl.loop(begin, end)
        def _(s):
            charge_of = quarter_valence(s)
            for x in range(BX):
                for y in range(0, BY, HALF):
                    rows = slice(x * BY + y, x * BY + y + HALF)
                    centre, spread, diff = differences(l0, s, x, y)
                    diffusion = dif[s, rows, :]
                    scaled = charge_of * diffusion
                    total = centre + diffusion * spread
                    for axis in range(3):
                        total = total + (0.5 * vel[axis, rows, :]) * diff[axis]
                        grad[axis, s, rows, :] = scaled * diff[axis]
                    base[s, rows, :] = total

    def load_rest():
        for load in loads[3:]:
            load.wait()

    ahead = mz < 4
    behind = jnp.logical_not(ahead)

    @pl.when(ahead)
    def _():
        pack_first()
        load_rest()
        first_own(0, SPECIES)

    pl.semaphore_wait(
        barrier,
        NYZ - 1 + has["x+"].astype(jnp.int32) + has["x-"].astype(jnp.int32),
    )

    @pl.when(middle)
    def _():
        pl.semaphore_signal(group_in, inc=1, device_id={"gx": far_gx}, device_id_type=MESH)

    def part(ref, index, start, count):
        return ref.at[pl.ds(index * TILE + start, count), :]

    def send_part(number, start, count):
        def act(peer):
            pltpu.make_async_remote_copy(
                src_ref=part(sendbuf, peer, start, count),
                dst_ref=part(recv, me, start, count),
                send_sem=a2a_send.at[number], recv_sem=a2a_recv.at[number],
                device_id={"yz": peer}, device_id_type=MESH,
            ).start()
        return act

    def bytes_of(ref, rows, sem):
        return pltpu.make_async_copy(ref.at[pl.ds(0, rows), :], ref.at[pl.ds(0, rows), :], sem)

    first, last = me == 0, me == NYZ - 1
    special = first | last

    def edge_tile(peer, side):
        return pltpu.make_async_remote_copy(
            src_ref=part(sendbuf, peer, FACE, TILE - FACE), dst_ref=part(recv, me, FACE, TILE - FACE),
            send_sem=edge_send, recv_sem=edge_recv.at[side],
            device_id={"yz": peer}, device_id_type=MESH,
        )

    def pass_on(side):
        return pltpu.make_async_remote_copy(
            src_ref=part(recv, (NYZ - 1) * (1 - side), 0, BX), dst_ref=part(recv, LOW + side, 0, BX),
            send_sem=pass_send.at[side], recv_sem=pass_recv.at[side],
            device_id=ids["y-" if side else "y+"], device_id_type=MESH,
        )

    mine = pl.ds(me * TILE, TILE)
    recv[mine, :] = sendbuf[mine, :]
    partners(send_part(0, 0, FACE))
    pl.when(last)(lambda: partners(lambda peer: edge_tile(peer, 0).start()))
    pl.when(first)(lambda: partners(lambda peer: edge_tile(peer, 1).start()))

    pl.when(behind)(pack_first)
    send_lanes(0, l0, lambda s: packs[s])
    start(0, l0, ("x+", "x-"))
    send_rows(0, l0)
    def far_row(side):
        def act(peer):
            pltpu.make_async_remote_copy(
                src_ref=part(sendbuf, peer, PLACE[0 if side else BX - 1], 1),
                dst_ref=pot_in.at[side, 0, pl.ds(me, 1), :],
                send_sem=far_send, recv_sem=far_recv,
                device_id={"gx": far_gx, "yz": peer}, device_id_type=MESH,
            ).start()
        return act

    def send_far(side):
        partners(far_row(side))
        far_row(side)(me)

    @pl.when(middle)
    def _():
        pl.semaphore_wait(group_in, 1)

    pl.when(lower)(lambda: send_far(0))
    pl.when(upper)(lambda: send_far(1))

    pl.when(jnp.logical_not(special) & ahead)(lambda: partners(send_part(1, FACE, TILE - FACE)))

    @pl.when(behind)
    def _():
        load_rest()
        first_own(0, SPECIES)

    pl.when(jnp.logical_not(special) & behind)(lambda: partners(send_part(1, FACE, TILE - FACE)))

    bytes_of(recv, (NYZ - 1) * FACE, a2a_recv.at[0]).wait()

    def assemble(x):
        pot[0, padded_row(x) : padded_row(x) + BY, :] = recv[pl.ds(PLACE[x], BY, stride=TILE), :]

    assemble(0)
    assemble(BX - 1)
    pl.when(jnp.logical_not(lower))(lambda: start(STEPS, pot, ("x+",)))
    pl.when(jnp.logical_not(upper))(lambda: start(STEPS, pot, ("x-",)))
    pl.when(jnp.logical_not(last))(lambda: edge_tile(lax.rem(me + 1, NYZ), 0).wait_recv())
    pl.when(jnp.logical_not(first))(lambda: edge_tile(lax.rem(me + 1, NYZ), 1).wait_recv())
    pl.when(has["y+"])(lambda: pass_on(0).start())
    pl.when(has["y-"])(lambda: pass_on(1).start())

    def rim_terms(axis, side, s, rows):
        diffusion, flow = dif[s, rows, :], 0.5 * vel[axis, rows, :]
        scaled = quarter_valence(s) * diffusion
        if side == 0:
            return diffusion - flow, -scaled
        return diffusion + flow, scaled

    receive(0, l0, ("x+", "x-", "y+", "y-"))
    receive_lanes(0, l0)

    @pl.loop(0, SPECIES)
    def _(s):
        for side in (0, 1):
            x = (BX - 1) * side
            rows = slice(x * BY, (x + 1) * BY)
            value = x_in[0, side, s]
            to_base, to_grad = rim_terms(0, side, s, rows)
            base[s, rows, :] += to_base * value
            grad[0, s, rows, :] += to_grad * value
            rows = pl.ds((BY - 1) * side, BX, stride=BY)
            value = y_in[0, side, s]
            to_base, to_grad = rim_terms(1, side, s, rows)
            base[s, rows, :] += to_base * value
            grad[1, s, rows, :] += to_grad * value
        for x, r in EVERY:
            rows = slice(x * BY + 8 * r, x * BY + 8 * r + 8)
            value = unpack(came[s], x, r)
            diffusion, flow = dif[s, rows, :], 0.5 * vel[2, rows, :]
            scaled = quarter_valence(s) * diffusion
            base[s, rows, :] += (diffusion + jnp.where(tile_low, -flow, flow)) * value
            grad[2, s, rows, :] += jnp.where(tile_low, -scaled, scaled) * value

    pl.when(special)(
        lambda: bytes_of(recv, (NYZ - 2) * (TILE - FACE), a2a_recv.at[1]).wait()
    )
    pl.when(jnp.logical_not(special))(
        lambda: bytes_of(recv, (NYZ - 3) * (TILE - FACE), a2a_recv.at[1]).wait()
    )
    for x in range(1, BX - 1):
        assemble(x)
    z_rims = pltpu.roll(recv[pl.ds(BX, BY, stride=TILE), :], (BZ - p) & (BZ - 1), 1)

    def first_step(x):
        rims_here = pltpu.roll(z_rims, BZ - 16 * x, 1) if x else z_rims
        for y in range(0, BY, HALF):
            r = padded_row(x) + y
            rows = slice(x * BY + y, x * BY + y + HALF)
            centre = pot[0, r : r + HALF, :]
            rim = rims_here[y : y + HALF]
            z_plus = jnp.where(half_high, rim, pltpu.roll(centre, BZ - 1, 1))
            z_minus = jnp.where(half_low, rim, pltpu.roll(centre, 1, 1))
            here = (
                pot[0, r + ROWS : r + ROWS + HALF, :] - pot[0, r - ROWS : r - ROWS + HALF, :],
                pot[0, r + 1 : r + 1 + HALF, :] - pot[0, r - 1 : r - 1 + HALF, :],
                z_plus - z_minus,
            )
            for axis in range(3):
                slope[axis, rows, :] = here[axis]
            for s in range(SPECIES):
                total = base[s, rows, :]
                for axis in range(3):
                    total = total - here[axis] * grad[axis, s, rows, :]
                l1[s, r : r + HALF, :] = total

    for x in range(BX):
        first_step(x)
    packed = [pack(line, own_tiles(l1, s), INNER) for s in range(SPECIES)]
    pl.when(has["y-"])(lambda: pass_on(0).wait_recv())
    pl.when(has["y+"])(lambda: pass_on(1).wait_recv())
    for side in (0, 1):
        at = (LOW + side) * TILE
        change = pltpu.roll(recv[at : at + BX, :], BX - 1, 0)
        change = change if side else -change
        rows = pl.ds((BY - 1) * side, BX, stride=BY)
        padded_rows = pl.ds(padded_row(0) + (BY - 1) * side, BX, stride=ROWS)
        slope[1, rows, :] += change
        for s in range(SPECIES):
            l1[s, padded_rows, :] -= change * grad[1, s, rows, :]
    packed = [pack(packed[s], own_tiles(l1, s), EDGES) for s in range(SPECIES)]
    pl.when(jnp.logical_not(upper))(lambda: receive(STEPS, pot, ("x+",)))
    pl.when(jnp.logical_not(lower))(lambda: receive(STEPS, pot, ("x-",)))
    pl.when(middle)(lambda: bytes_of(sendbuf, BY, far_recv).wait())
    for side in (0, 1):
        x = (BX - 1) * side
        change = -pot_in[side, 0] if side else pot_in[side, 0]
        rows = slice(x * BY, (x + 1) * BY)
        for s in range(SPECIES):
            l1[s, padded_row(x) : padded_row(x) + BY, :] += change * grad[0, s, rows, :]
    packed = [pack(packed[s], own_tiles(l1, s), FACES) for s in range(SPECIES)]
    send_lanes(1, l1, lambda s: packed[s])
    for s in range(SPECIES):
        side_out[s] = packed[s]
    start(1, l1, ("l+", "l-"))
    start(1, l1, ("x+", "x-"))
    send_rows(1, l1)
    for side in (0, 1):
        rows = slice((BX - 1) * side * BY, ((BX - 1) * side + 1) * BY)
        slope[0, rows, :] += pot_in[side, 0] if side else -pot_in[side, 0]

    def own_values(step, now, later, row_of):
        @pl.loop(0, SPECIES)
        def _(s):
            charge_of = quarter_valence(s)
            for x in range(BX):
                for y in range(0, BY, HALF):
                    rows = slice(x * BY + y, x * BY + y + HALF)
                    centre, spread, diff = differences(now, s, x, y)
                    diffusion = dif[s, rows, :]
                    total = centre + diffusion * spread
                    scaled = charge_of * diffusion
                    for axis in range(3):
                        if step == 1:
                            rate = 0.5 * vel[axis, rows, :] - scaled * slope[axis, rows, :]
                            along[axis, s, rows, :] = rate
                        else:
                            rate = along[axis, s, rows, :]
                        total = total + rate * diff[axis]
                    r = row_of(x) + y
                    later[s, r : r + HALF, :] = total

    def x_values(step, later, row_of):
        for s in range(SPECIES):
            for side in (0, 1):
                x = (BX - 1) * side
                rows = slice(x * BY, (x + 1) * BY)
                rate = along[0, s, rows, :]
                factor = dif[s, rows, :] + (rate if side else -rate)
                later[s, row_of(x) : row_of(x) + BY, :] += factor * x_in[step, side, s]

    def y_values(step, later, row_of):
        apart = row_of(1) - row_of(0)
        for s in range(SPECIES):
            for side in (0, 1):
                rows = pl.ds((BY - 1) * side, BX, stride=BY)
                rate = along[1, s, rows, :]
                factor = dif[s, rows, :] + (rate if side else -rate)
                later[s, pl.ds(row_of(0) + (BY - 1) * side, BX, stride=apart), :] += factor * y_in[step, side, s]

    def lane_factor(s):
        def tile_of(x, r):
            rows = slice(x * BY + 8 * r, x * BY + 8 * r + 8)
            rate = along[2, s, rows, :]
            return dif[s, rows, :] + jnp.where(tile_low, -rate, rate)
        return tile_of

    def lane_values(s, places, later, row_of):
        factor = lane_factor(s)
        for x, r in places:
            row = row_of(x) + 8 * r
            later[s, row : row + 8, :] += factor(x, r) * unpack(came[s], x, r)

    def by_pairs(act):
        @pl.loop(0, SPECIES // 2)
        def _(pair):
            act(2 * pair)
            act(2 * pair + 1)

    own_values(1, l1, l2, padded_row)

    def pack_factors(s):
        factors[s] = pack(line, lane_factor(s), EVERY)

        def x_factor(x, r):
            rows = slice(x * BY + 8 * r, x * BY + 8 * r + 8)
            rate = along[0, s, rows, :]
            return dif[s, rows, :] + (rate if x else -rate)

        x_factors[s] = pack(line, x_factor, FACES)

    by_pairs(pack_factors)
    packed = [pack(line, own_tiles(l2, s), INNER) for s in range(SPECIES)]
    receive(1, l1, ("y+", "y-"))
    y_values(1, l2, padded_row)
    packed = [pack(packed[s], own_tiles(l2, s), OUTER) for s in range(SPECIES)]
    receive(1, l1, ("l+", "l-"))
    slab = ((lanes() + 1) >> 4) & (BX - 1)

    def beside(s):
        low, high = pltpu.roll(side_in[0, s], 16, 1), pltpu.roll(side_in[1, s], BZ - 16, 1)
        return jnp.where(slab == 0, low, jnp.where(slab == BX - 1, high, 0.0))

    packed = [packed[s] + x_factors[s] * beside(s) for s in range(SPECIES)]
    receive_lanes(1, l1)
    send_lanes(2, l2, lambda s: packed[s] + factors[s] * came[s])
    receive(1, l1, ("x+", "x-"))
    x_values(1, l2, padded_row)
    for s in range(SPECIES):
        lane_values(s, FACES, l2, padded_row)
    start(2, l2, ("x+", "x-"))
    for s in range(SPECIES):
        lane_values(s, EDGES, l2, padded_row)
    send_rows(2, l2)
    by_pairs(lambda s: lane_values(s, INNER, l2, padded_row))

    flat_row = lambda x: x * BY
    own_values(2, l2, l3, flat_row)
    receive(2, l2, ("y+", "y-"))
    y_values(2, l3, flat_row)
    receive_lanes(2, l2)

    by_pairs(lambda s: lane_values(s, EVERY, l3, flat_row))
    receive(2, l2, ("x+", "x-"))
    x_values(2, l3, flat_row)

    @pl.when(special)
    def _():
        bytes_of(sendbuf, (NYZ - 1) * (TILE - FACE), edge_send).wait()

    bytes_of(sendbuf, (NYZ - 1) * FACE, a2a_send.at[0]).wait()

    @pl.when(jnp.logical_not(special))
    def _():
        bytes_of(sendbuf, (NYZ - 1) * (TILE - FACE), a2a_send.at[1]).wait()

    pl.when(has["y+"])(lambda: pass_on(0).wait_send())
    pl.when(has["y-"])(lambda: pass_on(1).wait_send())
    for stage, ref in enumerate((l0, l1, l2)):
        finish(stage, ref)
    finish(1, l1, ("l+", "l-"))
    pl.when(jnp.logical_not(lower))(lambda: finish(STEPS, pot, ("x+",)))
    pl.when(jnp.logical_not(upper))(lambda: finish(STEPS, pot, ("x-",)))
    pl.when(middle)(lambda: bytes_of(sendbuf, BY, far_send).wait())


def hand_over_kernel(source, target, sems):
    copies = [
        pltpu.make_async_copy(source.at[s], target.at[s], sems.at[s]) for s in range(SPECIES)
    ]
    for copy in copies:
        copy.start()
    for copy in copies:
        copy.wait()


def body(terminal_adjoint, diffusivity, velocity, charge_modes):
    high, low = base_table()
    cells = BX * BY
    brick = (SPECIES, cells, BZ)
    padded = (SPECIES, (BX + 2) * ROWS, BZ)
    flow = (3, cells, BZ)
    anywhere = pl.BlockSpec(memory_space=pl.ANY)
    out = pl.pallas_call(
        slab_kernel,
        out_shape=pltpu.VMEM(brick, F32),
        in_specs=[anywhere] * 6,
        out_specs=pl.BlockSpec(memory_space=pltpu.VMEM),
        scratch_shapes=[
            pltpu.VMEM(padded, F32), pltpu.VMEM(padded, F32), pltpu.VMEM(padded, F32),
            pltpu.VMEM(brick, F32),
            pltpu.VMEM(flow, F32),
            pltpu.VMEM((3,) + brick, F32),
            pltpu.VMEM(brick, F32),
            pltpu.VMEM((3,) + brick, F32),
            pltpu.VMEM(flow, F32),
            pltpu.VMEM((1,) + padded[1:], F32),
            pltpu.VMEM((BX, PY, MODES), F32),
            pltpu.VMEM((MODES, BZ), BF16), pltpu.VMEM((MODES, BZ), BF16),
            pltpu.VMEM((PZ, BX * PY, BZ), F32),
            pltpu.VMEM((NYZ * TILE, BZ), F32),
            pltpu.VMEM(((NYZ + 2) * TILE, BZ), F32),
            pltpu.VMEM((STEPS, 2, SPECIES, BY, BZ), F32),
            pltpu.VMEM((STEPS, 2, SPECIES, BX, BZ), F32),
            pltpu.VMEM((STEPS, 2, SPECIES, BX, BZ), F32),
            pltpu.VMEM((STEPS, 2, SPECIES // 2, 8, BZ), F32),
            pltpu.VMEM((STEPS, 2, SPECIES // 2, 8, BZ), F32),
            pltpu.VMEM((2, 1, BY, BZ), F32),
            pltpu.VMEM((SPECIES, 8, BZ), F32),
            pltpu.VMEM((2, SPECIES, 8, BZ), F32),
            pltpu.VMEM((SPECIES, 8, BZ), F32),
            pltpu.VMEM((SPECIES, 8, BZ), F32),
            pltpu.VMEM((SPECIES, 8, BZ), F32),
            pltpu.VMEM((SPECIES, 8, BZ), F32),
            pltpu.SemaphoreType.DMA((5,)),
            pltpu.SemaphoreType.DMA((BX,)),
            pltpu.SemaphoreType.DMA((2,)),
            pltpu.SemaphoreType.DMA((2,)),
            pltpu.SemaphoreType.DMA,
            pltpu.SemaphoreType.DMA((2,)),
            pltpu.SemaphoreType.DMA((2,)),
            pltpu.SemaphoreType.DMA((2,)),
            pltpu.SemaphoreType.REGULAR,
            pltpu.SemaphoreType.DMA,
            pltpu.SemaphoreType.DMA,
            pltpu.SemaphoreType.DMA((STEPS + 1, 8)),
            pltpu.SemaphoreType.DMA((STEPS + 1, 8)),
        ],
        compiler_params=pltpu.CompilerParams(
            collective_id=0, has_side_effects=True, vmem_limit_bytes=60 * 1024 * 1024
        ),
    )(
        terminal_adjoint.reshape(SPECIES, BX, BY, BZ),
        diffusivity.reshape(brick),
        velocity.reshape(flow),
        charge_modes.reshape(BX, PY, MODES),
        jnp.asarray(high),
        jnp.asarray(low),
    )
    return out.reshape(terminal_adjoint.shape)


def solution(mesh):
    return jax.shard_map(
        body,
        mesh=mesh,
        in_specs=(
            P(None, "gx", None, "yz", None),
            P(None, "gx", None, "yz", None),
            P(None, "gx", None, "yz", None),
            P("gx", "yz", None, None),
        ),
        out_specs=P(None, "gx", None, "yz", None),
        check_vma=False,
    )
```
